32 devices in a mesh: panel: 2 (over core), lon: 8 (over z, x), lat: 2 (over y).
Axes of the slice: x: 2, y: 2, z: 4, core: 2. Of those that a mesh axis runs over, the one named last changes fastest.
Arguments:
- fields: float32 [2, 24, 256, 256], P('panel', None, 'lon', 'lat'), may hold values from -6 to 6
- offsets: int32 [2, 2, 32, 2], P('panel', None, 'lon', 'lat'), may hold values from -7 to 7
- fractions: float32 [2, 2, 256, 256], P('panel', None, 'lon', 'lat'), may hold values from 0 to 1
- send_count: int32 [2, 8, 2], P('panel', 'lon', 'lat'), may hold values from 0 to 64, as said below
- send_owner: int32 [2, 8, 2, 64], P('panel', 'lon', 'lat'), may hold values from 0 to 7, as said below
- send_cell: int32 [2, 8, 2, 64], P('panel', 'lon', 'lat'), may hold values from 0 to 3966, as said below
- send_target: int32 [2, 8, 2, 64], P('panel', 'lon', 'lat'), may hold values from 0 to 127, as said below
- send_frac: float32 [2, 8, 2, 2, 64], P('panel', 'lon', 'lat'), may hold values from 0 to 1
Outputs:
- advected_fields: float32 [2, 24, 256, 256], P('panel', None, 'lon', 'lat')
The draws below stay inside these ranges and needn't reach their ends.
Inputs may be any that keep to these rules, and one draw needn't show every extreme that they name: `send_count`: 64 on the devices that give donor values and 0 elsewhere; in each row of devices along longitude (one panel, one latitude index) the donors are the first 4 or the last 4 longitude indices. `send_owner`: the receiving device lies on the other panel at the same latitude index and is at the first or the last longitude index; the live slots of a donor name each of the two exactly 32 times. `send_cell`: lon_row * 128 + lat_col with lon_row < 31 and lat_col < 127. `send_target`: over the live slots of all donors that fill one receiving device, every value from 0 to 127 appears exactly once.
All inputs are finite; a program needn't handle non-finite values.
Results may differ from the reference program's by a relative error of at most 0.00002.
Values sent between devices are 32-bit elements; how exact they have to be, the bound alone decides.
A program may use at most 64 MiB of HBM per device.

```python
import jax
import jax.numpy as jnp
from jax import lax

FIELDS = 6
LEVELS = 4
CLON = 32
CLAT = 128
TILE = 8
BLOCK = 128
REACH = 7
HALO = 9
NLON = 256
NLAT = 256
BAND = 4
CAP = 32
SLOTS = 64
N_LON = 8
N_LAT = 2


def border_plan(key):
    lon_count = NLON // CLON
    lat_count = NLAT // CLAT
    band_key, perm_key, shuffle_key = jax.random.split(key, 3)
    band_start = (jax.random.randint(band_key, (2, lat_count), 0, 2) * (lon_count - BAND)).astype(jnp.int32)
    perm_keys = jax.random.split(perm_key, 2 * lat_count * 2)
    rim_perms = jax.vmap(lambda k: jax.random.permutation(k, CLAT))(perm_keys).reshape(2, lat_count, 2, CLAT).astype(jnp.int32)
    shuffle_keys = jax.random.split(shuffle_key, 2 * lon_count * lat_count)
    shuffles = jax.vmap(lambda k: jax.random.permutation(k, SLOTS))(shuffle_keys).reshape(2, lon_count, lat_count, SLOTS).astype(jnp.int32)
    donor_panel = jnp.arange(2, dtype=jnp.int32)[:, None, None]
    lon_index = jnp.arange(lon_count, dtype=jnp.int32)[None, :, None]
    lat_index = jnp.arange(lat_count, dtype=jnp.int32)[None, None, :]
    recv_panel = 1 - donor_panel
    position = lon_index - band_start[recv_panel, lat_index]
    is_live = (position >= 0) & (position < BAND)
    live_count = jnp.where(is_live, SLOTS, 0).astype(jnp.int32)
    slot_index = jnp.arange(SLOTS, dtype=jnp.int32)
    rim_side = slot_index // CAP
    within = slot_index % CAP
    donor_slot = jnp.clip(position, 0, BAND - 1)[..., None] * CAP + within
    target = rim_perms[recv_panel[..., None], lat_index[..., None], rim_side, donor_slot]
    owner_lon = jnp.broadcast_to(rim_side * (lon_count - 1), target.shape).astype(jnp.int32)
    target = jnp.take_along_axis(target, shuffles, axis=-1)
    owner_lon = jnp.take_along_axis(owner_lon, shuffles, axis=-1)
    return (live_count, owner_lon, target)


def draw_send_count(key, part):
    return border_plan(key)[0]


def draw_send_owner(key, part):
    return border_plan(key)[1]


def draw_send_target(key, part):
    return border_plan(key)[2]


def draw_send_cell(key, part):
    key = jax.random.fold_in(key, 7)
    lon_count = NLON // CLON
    lat_count = NLAT // CLAT
    row_key, col_key = jax.random.split(key)
    shape = (2, lon_count, lat_count, SLOTS)
    cell_row = jax.random.randint(row_key, shape, 0, CLON - 1)
    cell_col = jax.random.randint(col_key, shape, 0, CLAT - 1)
    cell_row = cell_row.at[0, 0, 0, 0].set(0).at[0, 0, 0, 1].set(CLON - 2)
    cell_col = cell_col.at[0, 0, 0, 0].set(0).at[0, 0, 0, 1].set(CLAT - 2)
    return (cell_row * CLAT + cell_col).astype(jnp.int32)


def touch_ends(array, own_key, low, top_value):
    index_at = [jax.random.randint(jax.random.fold_in(own_key, axis), (), 0, length) for axis, length in enumerate(array.shape)]
    widest = array.shape.index(max(array.shape))
    neighbour = index_at[:widest] + [(index_at[widest] + 1) % array.shape[widest]] + index_at[widest + 1:]
    return array.at[tuple(index_at)].set(low).at[tuple(neighbour)].set(top_value)


def block_levels(rng, dims, cuts, low, largest):
    loudness, own = 1.0, jax.random.fold_in(rng, 6)
    for dim, shards_of in cuts:
        steps = jnp.exp(jax.random.uniform(jax.random.fold_in(own, dim), (shards_of,), jnp.float32, low / len(cuts), largest / len(cuts)))
        loudness = loudness * jnp.repeat(steps, dims[dim] // shards_of).reshape([-1 if axis == dim else 1 for axis in range(len(dims))])
    return loudness


def scatter_about(stream_key, shape, width, reach, shards=(), held_as=jnp.bfloat16):
    array = width * jax.random.normal(stream_key, shape, jnp.float32)
    if shards:
        array = array * block_levels(stream_key, shape, shards, -0.22, 0.18)
    return jnp.clip(array, -reach, reach).astype(held_as)


def setup_inputs(seed: int = 0) -> dict:
    seeds = jax.random.split(jax.random.key(seed), 9)
    return {
        "fields": scatter_about(seeds[0], (2, FIELDS * LEVELS, NLON, NLAT), 1.0, 6.0, ((0, 2), (2, 8), (3, 2)), jnp.float32),
        "offsets": touch_ends(jax.random.randint(seeds[1], (2, 2, NLON // TILE, NLAT // BLOCK), -REACH, REACH + 1), jax.random.fold_in(seeds[1], 1), -REACH, REACH).astype(jnp.int32),
        "fractions": jnp.clip(1.0 * jax.random.uniform(seeds[2], (2, 2, NLON, NLAT), jnp.float32) ** block_levels(seeds[2], (2, 2, NLON, NLAT), ((0, 2), (2, 8), (3, 2)), -0.2, 0.2), 0.0, 1.0),
        "send_count": draw_send_count(jax.random.fold_in(seeds[8], 71), 0),
        "send_owner": draw_send_owner(jax.random.fold_in(seeds[8], 71), 0),
        "send_cell": draw_send_cell(jax.random.fold_in(seeds[8], 71), 0),
        "send_target": draw_send_target(jax.random.fold_in(seeds[8], 71), 0),
        "send_frac": jnp.clip(1.0 * jax.random.uniform(seeds[7], (2, N_LON, N_LAT, 2, SLOTS), jnp.float32) ** block_levels(seeds[7], (2, N_LON, N_LAT, 2, SLOTS), ((0, 2), (1, 8), (2, 2)), -0.2, 0.2), 0.0, 1.0),
    }


def lagrange(x):
    return (-x * (x - 1.0) * (x - 2.0) / 6.0, (x + 1.0) * (x - 1.0) * (x - 2.0) / 2.0,
            -(x + 1.0) * x * (x - 2.0) / 2.0, (x + 1.0) * x * (x - 1.0) / 6.0)


def interpolate(window, frac_lon, frac_lat):
    lon_weights = lagrange(frac_lon)
    lat_weights = lagrange(frac_lat)
    summed = jnp.zeros((window.shape[0], TILE, BLOCK), jnp.float32)
    for a in range(4):
        inner_sum = jnp.zeros((window.shape[0], TILE, BLOCK), jnp.float32)
        for b in range(4):
            inner_sum = inner_sum + lat_weights[b] * window[:, a:a + TILE, b:b + BLOCK]
        summed = summed + lon_weights[a] * inner_sum
    return summed


def advect(padded, offsets, fractions, halo_width):
    tiles_lon = offsets.shape[1]
    tiles_lat = offsets.shape[2]
    channels = padded.shape[0]

    def one_row(t):
        def one_tile(u):
            start_lon = t * TILE + halo_width + offsets[0, t, u] - 1
            start_lat = u * BLOCK + halo_width + offsets[1, t, u] - 1
            window = lax.dynamic_slice(padded, (jnp.int32(0), start_lon, start_lat), (channels, TILE + 3, BLOCK + 3))
            frac_tile = lax.dynamic_slice(fractions, (jnp.int32(0), t * TILE, u * BLOCK), (2, TILE, BLOCK))
            return interpolate(window, frac_tile[0], frac_tile[1])
        return jax.vmap(one_tile)(jnp.arange(tiles_lat, dtype=jnp.int32))

    tiled = lax.map(one_row, jnp.arange(tiles_lon, dtype=jnp.int32))
    return tiled.transpose(2, 0, 3, 1, 4).reshape(channels, tiles_lon * TILE, tiles_lat * BLOCK)


def bilinear(base_val, lat_next, lon_next, diagonal_next, a, b):
    return (1.0 - a) * (1.0 - b) * base_val + (1.0 - a) * b * lat_next + a * (1.0 - b) * lon_next + a * b * diagonal_next


def reference(fields, offsets, fractions, send_count, send_owner, send_cell, send_target, send_frac):
    advected = jnp.stack([advect(jnp.pad(fields[p], ((0, 0), (HALO, HALO), (HALO, HALO))), offsets[p], fractions[p], HALO) for p in range(2)])
    lon_count = NLON // CLON
    lat_count = NLAT // CLAT
    slot_count = send_owner.shape[-1]
    panel_index = jnp.arange(2, dtype=jnp.int32)[:, None, None, None]
    lon_index = jnp.arange(lon_count, dtype=jnp.int32)[None, :, None, None]
    lat_index = jnp.arange(lat_count, dtype=jnp.int32)[None, None, :, None]
    src_row = lon_index * CLON + send_cell // CLAT
    src_col = lat_index * CLAT + send_cell % CLAT
    base_val = advected[panel_index, :, src_row, src_col]
    lat_next = advected[panel_index, :, src_row, src_col + 1]
    lon_next = advected[panel_index, :, src_row + 1, src_col]
    diagonal_next = advected[panel_index, :, src_row + 1, src_col + 1]
    frac_a = send_frac[:, :, :, 0, :][..., None]
    frac_b = send_frac[:, :, :, 1, :][..., None]
    donor = bilinear(base_val, lat_next, lon_next, diagonal_next, frac_a, frac_b)
    is_live = jnp.arange(slot_count, dtype=jnp.int32)[None, None, None, :] < send_count[..., None]
    dest_row = jnp.where(send_owner == 0, 0, NLON - 1).astype(jnp.int32)
    dest_col = jnp.where(is_live, lat_index * CLAT + send_target, NLAT).astype(jnp.int32)
    return advected.at[1 - panel_index, :, dest_row, dest_col].set(donor, mode="drop")
```

```python
import functools

import jax
import jax.numpy as jnp
from jax import lax
from jax.experimental import pallas as pl
from jax.experimental.pallas import tpu as pltpu
from jax.sharding import PartitionSpec as P

TILE = 8
LOW = 8
HIGH = 9
STRIP = 16
PER = 128 // STRIP
MESH = pl.DeviceIdType.MESH


def lagrange(x):
    return (
        -x * (x - 1.0) * (x - 2.0) * (1.0 / 6.0),
        (x + 1.0) * (x - 1.0) * (x - 2.0) * 0.5,
        -(x + 1.0) * x * (x - 2.0) * 0.5,
        (x + 1.0) * x * (x - 1.0) * (1.0 / 6.0),
    )


def kernel(
    lon_count, lat_count, rows, channels, slots,
    offsets, count, owner, cell, target, frac,
    x_ref, frac_ref, out_ref,
    ext, pack_l, pack_r, from_r, from_l, halo, weights, rim_out, rim_in,
    send_sem, recv_sem, rim_send, rim_recv,
):
    p = lax.axis_index("panel")
    i = lax.axis_index("lon")
    j = lax.axis_index("lat")
    groups = rows // PER
    has_prev, has_next = i > 0, i < lon_count - 1
    has_left, has_right = j > 0, j < lat_count - 1
    is_rim = jnp.logical_or(i == 0, i == lon_count - 1)

    own = LOW
    plan = [
        (ext.at[pl.ds(own, HIGH)], ext.at[pl.ds(own + rows, HIGH)], -1, 0, has_prev),
        (ext.at[pl.ds(own + rows - LOW, LOW)], ext.at[pl.ds(0, LOW)], 1, 0, has_next),
        (pack_l, from_r.at[pl.ds(1, groups)], 0, -1, has_left),
        (pack_r, from_l.at[pl.ds(1, groups)], 0, 1, has_right),
        (pack_l.at[pl.ds(0, 2)], from_r.at[pl.ds(1 + groups, 2)], -1, -1, has_prev & has_left),
        (pack_l.at[pl.ds(groups - 1, 1)], from_r.at[pl.ds(0, 1)], 1, -1, has_next & has_left),
        (pack_r.at[pl.ds(0, 2)], from_l.at[pl.ds(1 + groups, 2)], -1, 1, has_prev & has_right),
        (pack_r.at[pl.ds(groups - 1, 1)], from_l.at[pl.ds(0, 1)], 1, 1, has_next & has_right),
    ]
    arrives = [
        has_next, has_prev, has_right, has_left,
        has_next & has_right, has_prev & has_right, has_next & has_left, has_prev & has_left,
    ]

    barrier = pltpu.get_barrier_semaphore()
    waits = jnp.int32(0)
    for _, _, di, dj, there in plan:
        @pl.when(there)
        def _(di=di, dj=dj):
            pl.semaphore_signal(barrier, inc=1, device_id=(p, i + di, j + dj), device_id_type=MESH)
        waits = waits + there.astype(jnp.int32)

    @pl.when(is_rim)
    def _():
        def greet(m, carry):
            pl.semaphore_signal(barrier, inc=1, device_id=(1 - p, m, j), device_id_type=MESH)
            return carry
        lax.fori_loop(0, lon_count, greet, 0)

    @pl.when(jnp.logical_not(is_rim))
    def _():
        for m in (0, lon_count - 1):
            pl.semaphore_signal(barrier, inc=1, device_id=(1 - p, m, j), device_id_type=MESH)

    waits = waits + jnp.where(is_rim, lon_count, 2)

    def clear(ref, start, size):
        ref[pl.ds(start, size)] = jnp.zeros((size,) + ref.shape[1:], jnp.float32)

    @pl.when(jnp.logical_not(has_prev))
    def _():
        clear(ext, 0, LOW)
        clear(from_r, 0, 1)
        clear(from_l, 0, 1)

    @pl.when(jnp.logical_not(has_next))
    def _():
        clear(ext, own + rows, HIGH)
        clear(from_r, 1 + groups, 2)
        clear(from_l, 1 + groups, 2)

    @pl.when(jnp.logical_not(has_right))
    def _():
        clear(from_r, 0, groups + 3)

    @pl.when(jnp.logical_not(has_left))
    def _():
        clear(from_l, 0, groups + 3)

    lane = lax.broadcasted_iota(jnp.int32, (8, 128), 1)
    strip = lane // STRIP

    def prepare(g, carry):
        for c in range(channels // 8):
            left = jnp.zeros((8, 128), jnp.float32)
            right = jnp.zeros((8, 128), jnp.float32)
            for m in range(PER):
                row = g * PER + m
                v = x_ref[pl.ds(c * 8 * rows + row, 8, stride=rows), :]
                ext[own + row, pl.ds(c * 8, 8), :] = v
                rolled = pltpu.roll(v, STRIP * m, 1) if m else v
                left = jnp.where(strip == m, rolled, left)
                right = jnp.where(strip == (m + PER - 1) % PER, rolled, right)
            pack_l[g, pl.ds(c * 8, 8), :] = left
            pack_r[g, pl.ds(c * 8, 8), :] = right
        at = pl.ds(pl.multiple_of(g * 8, 8), 8)
        for axis in range(2):
            for n, w in enumerate(lagrange(frac_ref[axis, at, :])):
                weights[4 * axis + n, at, :] = w
        return carry

    lax.fori_loop(0, groups, prepare, 0)

    pl.semaphore_wait(barrier, waits)

    copies = []
    for n, (src, dst, di, dj, there) in enumerate(plan):
        copy = pltpu.make_async_remote_copy(
            src_ref=src, dst_ref=dst, send_sem=send_sem.at[n], recv_sem=recv_sem.at[n],
            device_id=(p, i + di, j + dj), device_id_type=MESH,
        )
        copies.append(copy)
        pl.when(there)(copy.start)
    for n, copy in enumerate(copies):
        pl.when(arrives[n])(copy.wait_recv)

    def unpack_row(g, m, c):
        at = pl.ds(c * 8, 8)
        a, b = from_r[g, at, :], from_l[g, at, :]
        if m:
            a = pltpu.roll(a, 128 - STRIP * m, 1)
            b = pltpu.roll(b, 128 - STRIP * m, 1)
        halo[g * PER + m, at, :] = jnp.where(lane < 64, a, b)

    def unpack(g, carry):
        for c in range(channels // 8):
            for m in range(PER):
                unpack_row(g, m, c)
        return carry

    lax.fori_loop(0, groups + 2, unpack, 0)
    for c in range(channels // 8):
        unpack_row(groups + 2, 0, c)

    wide = lax.broadcasted_iota(jnp.int32, (channels, 128), 1)

    def tile(t, carry):
        start = t * TILE + LOW - 1 + offsets[0, 0, t]
        shift = offsets[1, 0, t]
        inside, turn = [], []
        for b in range(4):
            k = shift + (b - 1)
            inside.append((wide >= k) & (wide < 128 + k))
            turn.append((256 - k) & 127)
        sums = [None] * TILE
        for q in range(TILE + 3):
            main, edge = ext[start + q], halo[start + q]
            shifted = [pltpu.roll(jnp.where(inside[b], main, edge), turn[b], 1) for b in range(4)]
            for a in range(4):
                r = q - a
                if not 0 <= r < TILE:
                    continue
                at = pl.ds(t * TILE + r, 1)
                inner = weights[4, at, :] * shifted[0]
                for b in range(1, 4):
                    inner = inner + weights[4 + b, at, :] * shifted[b]
                term = weights[a, at, :] * inner
                sums[r] = term if sums[r] is None else sums[r] + term
                if a == 3:
                    out_ref[t * TILE + r] = sums[r]
        return carry

    lax.fori_loop(0, rows // TILE, tile, 0)

    live = count[0, 0, 0]

    def donate(k, carry):
        first, last = carry
        place = cell[0, 0, 0, k]
        row, col = place >> 7, place & 127
        to = target[0, 0, 0, k]
        a, b = frac[0, 0, 0, 0, k], frac[0, 0, 0, 1, k]
        to_first = owner[0, 0, 0, k] == 0
        near, far = out_ref[row], out_ref[row + 1]
        here = (256 + to - col) & 127
        beyond = (255 + to - col) & 127
        near = (1.0 - b) * pltpu.roll(near, here, 1) + b * pltpu.roll(near, beyond, 1)
        far = (1.0 - b) * pltpu.roll(far, here, 1) + b * pltpu.roll(far, beyond, 1)
        value = (1.0 - a) * near + a * far
        to = jnp.where(k < live, to, 128)
        first = jnp.where(wide == jnp.where(to_first, to, 128), value, first)
        last = jnp.where(wide == jnp.where(to_first, 128, to), value, last)
        return first, last

    zero = jnp.zeros((channels, 128), jnp.float32)
    first, last = lax.fori_loop(0, slots, donate, (zero, zero))
    rim_out[0] = first
    rim_out[1] = last

    sends = []
    for n, m in enumerate((0, lon_count - 1)):
        copy = pltpu.make_async_remote_copy(
            src_ref=rim_out.at[n], dst_ref=rim_in.at[i], send_sem=rim_send.at[n],
            recv_sem=rim_recv.at[i], device_id=(1 - p, m, j), device_id_type=MESH,
        )
        copy.start()
        sends.append(copy)

    @pl.when(is_rim)
    def _():
        total = zero
        for m in range(lon_count):
            pltpu.make_async_remote_copy(
                src_ref=rim_out.at[0], dst_ref=rim_in.at[m], send_sem=rim_send.at[0],
                recv_sem=rim_recv.at[m], device_id=(1 - p, m, j), device_id_type=MESH,
            ).wait_recv()
            total = total + rim_in[m]
        out_ref[jnp.where(i == 0, 0, rows - 1)] = total

    for n, copy in enumerate(copies):
        pl.when(plan[n][4])(copy.wait_send)
    for copy in sends:
        copy.wait_send()


def body(fields, offsets, fractions, send_count, send_owner, send_cell, send_target, send_frac):
    _, channels, rows, columns = fields.shape
    lon_count, lat_count = lax.axis_size("lon"), lax.axis_size("lat")
    slots = send_owner.shape[-1]
    groups = rows // PER
    smem = pl.BlockSpec(memory_space=pltpu.SMEM)
    vmem = pl.BlockSpec(memory_space=pltpu.VMEM)
    f32 = jnp.float32
    out = pl.pallas_call(
        functools.partial(kernel, lon_count, lat_count, rows, channels, slots),
        out_shape=jax.ShapeDtypeStruct((rows, channels, columns), f32),
        in_specs=[smem] * 6 + [vmem] * 2,
        out_specs=vmem,
        scratch_shapes=[
            pltpu.VMEM((LOW + rows + HIGH, channels, columns), f32),
            pltpu.VMEM((groups, channels, columns), f32),
            pltpu.VMEM((groups, channels, columns), f32),
            pltpu.VMEM((groups + 3, channels, columns), f32),
            pltpu.VMEM((groups + 3, channels, columns), f32),
            pltpu.VMEM((LOW + rows + HIGH, channels, columns), f32),
            pltpu.VMEM((8, rows, columns), f32),
            pltpu.VMEM((2, channels, columns), f32),
            pltpu.VMEM((lon_count, channels, columns), f32),
            pltpu.SemaphoreType.DMA((8,)),
            pltpu.SemaphoreType.DMA((8,)),
            pltpu.SemaphoreType.DMA((2,)),
            pltpu.SemaphoreType.DMA((lon_count,)),
        ],
        compiler_params=pltpu.CompilerParams(
            collective_id=0, has_side_effects=True, vmem_limit_bytes=24 * 1024 * 1024
        ),
    )(
        offsets.reshape(2, 1, rows // TILE), send_count, send_owner, send_cell, send_target, send_frac,
        fields.reshape(channels * rows, columns), fractions.reshape(2, rows, columns),
    )
    return out.transpose(1, 0, 2)[None]


def solution(mesh):
    placed = (
        P("panel", None, "lon", "lat"),
        P("panel", None, "lon", "lat"),
        P("panel", None, "lon", "lat"),
        P("panel", "lon", "lat"),
        P("panel", "lon", "lat", None),
        P("panel", "lon", "lat", None),
        P("panel", "lon", "lat", None),
        P("panel", "lon", "lat", None, None),
    )
    return jax.shard_map(
        body, mesh=mesh, in_specs=placed, out_specs=P("panel", None, "lon", "lat"), check_vma=False
    )
```

```python
import functools

import jax
import jax.numpy as jnp
from jax import lax
from jax.experimental import pallas as pl
from jax.experimental.pallas import tpu as pltpu
from jax.sharding import PartitionSpec as P

TILE = 8
LOW = 8
HIGH = 9
STRIP = 16
PER = 128 // STRIP
MESH = pl.DeviceIdType.MESH


def lagrange(x):
    return (
        -x * (x - 1.0) * (x - 2.0) * (1.0 / 6.0),
        (x + 1.0) * (x - 1.0) * (x - 2.0) * 0.5,
        -(x + 1.0) * x * (x - 2.0) * 0.5,
        (x + 1.0) * x * (x - 1.0) * (1.0 / 6.0),
    )


def kernel(
    lon_count, lat_count, rows, channels, slots,
    offsets_hbm, count, owner_hbm, cell_hbm, target_hbm, frac_hbm, x_hbm, fractions_hbm, out_ref,
    offsets, owner, cell, target, frac, x_ref, frac_ref,
    ext, land_lo, land_hi, pack_l, pack_r, from_r, from_l, halo, weights, rim_out, rim_in,
    in_sem, send_sem, recv_sem, rim_send, rim_recv,
):
    p = lax.axis_index("panel")
    i = lax.axis_index("lon")
    j = lax.axis_index("lat")
    groups = rows // PER
    blocks = channels // 8
    own = LOW
    has_prev, has_next = i > 0, i < lon_count - 1
    has_left, has_right = j > 0, j < lat_count - 1
    is_rim = jnp.logical_or(i == 0, i == lon_count - 1)

    around = [
        (-1, 0, has_prev), (1, 0, has_next), (0, -1, has_left), (0, 1, has_right),
        (-1, -1, has_prev & has_left), (1, -1, has_next & has_left),
        (-1, 1, has_prev & has_right), (1, 1, has_next & has_right),
    ]
    barrier = pltpu.get_barrier_semaphore()
    waits = jnp.int32(0)
    for di, dj, there in around:
        @pl.when(there)
        def _(di=di, dj=dj):
            pl.semaphore_signal(barrier, inc=1, device_id=(p, i + di, j + dj), device_id_type=MESH)
        waits = waits + there.astype(jnp.int32)

    @pl.when(is_rim)
    def _():
        def greet(m, carry):
            pl.semaphore_signal(barrier, inc=1, device_id=(1 - p, m, j), device_id_type=MESH)
            return carry
        lax.fori_loop(0, lon_count, greet, 0)

    @pl.when(jnp.logical_not(is_rim))
    def _():
        for m in (0, lon_count - 1):
            pl.semaphore_signal(barrier, inc=1, device_id=(1 - p, m, j), device_id_type=MESH)

    waits = waits + jnp.where(is_rim, lon_count, 2)

    loads = [
        pltpu.make_async_copy(src, dst, in_sem.at[n])
        for n, (src, dst) in enumerate([
            (x_hbm, x_ref), (fractions_hbm, frac_ref), (offsets_hbm, offsets),
            (owner_hbm, owner), (cell_hbm, cell), (target_hbm, target), (frac_hbm, frac),
        ])
    ]
    for load in loads:
        load.start()

    def clear(ref, start, size):
        ref[pl.ds(start, size)] = jnp.zeros((size,) + ref.shape[1:], jnp.float32)

    @pl.when(jnp.logical_not(has_prev))
    def _():
        clear(land_lo, 0, LOW)
        clear(from_r, 0, 1)
        clear(from_l, 0, 1)

    @pl.when(jnp.logical_not(has_next))
    def _():
        clear(land_hi, 0, HIGH)
        clear(from_r, 1 + groups, 2)
        clear(from_l, 1 + groups, 2)

    @pl.when(jnp.logical_not(has_right))
    def _():
        clear(from_r, 0, groups + 3)

    @pl.when(jnp.logical_not(has_left))
    def _():
        clear(from_l, 0, groups + 3)

    lane = lax.broadcasted_iota(jnp.int32, (8, 128), 1)
    strip = lane // STRIP

    def turn_row(row, c):
        v = x_ref[pl.ds(c * 8 * rows + row, 8, stride=rows), :]
        ext[own + row, pl.ds(c * 8, 8), :] = v
        return v

    def pack(g):
        for c in range(blocks):
            left = jnp.zeros((8, 128), jnp.float32)
            right = jnp.zeros((8, 128), jnp.float32)
            for m in range(PER):
                v = ext[own + g * PER + m, pl.ds(c * 8, 8), :]
                rolled = pltpu.roll(v, STRIP * m, 1) if m else v
                left = jnp.where(strip == m, rolled, left)
                right = jnp.where(strip == (m + PER - 1) % PER, rolled, right)
            pack_l[g, pl.ds(c * 8, 8), :] = left
            pack_r[g, pl.ds(c * 8, 8), :] = right

    copies = []

    def send(src, dst, side):
        di, dj, there = around[side]
        n = len(copies)
        copy = pltpu.make_async_remote_copy(
            src_ref=src, dst_ref=dst, send_sem=send_sem.at[n], recv_sem=recv_sem.at[n],
            device_id=(p, i + di, j + dj), device_id_type=MESH,
        )
        arrives = [t for a, b, t in around if (a, b) == (-di, -dj)][0]
        copies.append((copy, there, arrives))
        pl.when(there)(copy.start)

    def arrive(n):
        copy, _, arrives = copies[n]
        pl.when(arrives)(copy.wait_recv)

    loads[0].wait()
    early = list(range(HIGH)) + list(range(rows - LOW, rows))
    for row in early:
        for c in range(blocks):
            turn_row(row, c)
    pl.semaphore_wait(barrier, waits)
    send(ext.at[pl.ds(own, 1)], land_hi.at[pl.ds(0, 1)], 0)
    send(ext.at[pl.ds(own + rows - LOW, LOW)], land_lo, 1)
    send(ext.at[pl.ds(own + 1, HIGH - 1)], land_hi.at[pl.ds(1, HIGH - 1)], 0)
    for row in range(HIGH, rows - LOW):
        for c in range(blocks):
            turn_row(row, c)
    for g in range(groups):
        pack(g)
    send(pack_l, from_r.at[pl.ds(1, groups)], 2)
    send(pack_r, from_l.at[pl.ds(1, groups)], 3)
    send(pack_l.at[pl.ds(0, 2)], from_r.at[pl.ds(1 + groups, 2)], 4)
    send(pack_l.at[pl.ds(groups - 1, 1)], from_r.at[pl.ds(0, 1)], 5)
    send(pack_r.at[pl.ds(0, 2)], from_l.at[pl.ds(1 + groups, 2)], 6)
    send(pack_r.at[pl.ds(groups - 1, 1)], from_l.at[pl.ds(0, 1)], 7)

    loads[1].wait()
    for g in range(groups):
        at = pl.ds(g * 8, 8)
        for axis in range(2):
            for n, w in enumerate(lagrange(frac_ref[axis, at, :])):
                weights[4 * axis + n, at, :] = w
    for load in loads[2:]:
        load.wait()

    def unpack(g, count):
        for c in range(blocks):
            at = pl.ds(c * 8, 8)
            for m in range(count):
                a, b = from_r[g, at, :], from_l[g, at, :]
                if m:
                    a = pltpu.roll(a, 128 - STRIP * m, 1)
                    b = pltpu.roll(b, 128 - STRIP * m, 1)
                halo[g * PER + m, at, :] = jnp.where(lane < 64, a, b)

    wide = lax.broadcasted_iota(jnp.int32, (channels, 128), 1)

    def tile(t):
        start = t * TILE + LOW - 1 + offsets[0, 0, t]
        shift = offsets[1, 0, t]
        inside, turn = [], []
        for b in range(4):
            k = shift + (b - 1)
            inside.append((wide >= k) & (wide < 128 + k))
            turn.append((256 - k) & 127)
        sums = [None] * TILE
        for q in range(TILE + 3):
            main, edge = ext[start + q], halo[start + q]
            shifted = [pltpu.roll(jnp.where(inside[b], main, edge), turn[b], 1) for b in range(4)]
            for a in range(4):
                r = q - a
                if not 0 <= r < TILE:
                    continue
                at = pl.ds(t * TILE + r, 1)
                inner = weights[4, at, :] * shifted[0]
                for b in range(1, 4):
                    inner = inner + weights[4 + b, at, :] * shifted[b]
                term = weights[a, at, :] * inner
                sums[r] = term if sums[r] is None else sums[r] + term
                if a == 3:
                    out_ref[t * TILE + r] = sums[r]

    tiles = rows // TILE
    for n in (3, 4):
        arrive(n)
    for g in range(1, 1 + groups):
        unpack(g, PER)
    for t in range(1, tiles - 2):
        tile(t)
    for n in (0, 5, 7):
        arrive(n)
    unpack(1 + groups, PER)
    unpack(2 + groups, 1)
    ext[own + rows] = land_hi[0]
    tile(tiles - 2)
    for n in (1, 6, 8):
        arrive(n)
    unpack(0, PER)
    ext[pl.ds(0, LOW)] = land_lo[...]
    tile(0)
    arrive(2)
    ext[pl.ds(own + rows + 1, HIGH - 1)] = land_hi[pl.ds(1, HIGH - 1)]
    tile(tiles - 1)

    live = count[0, 0, 0]

    def donate(k, carry):
        first, last = carry
        place = cell[0, 0, 0, k]
        row, col = place >> 7, place & 127
        to = target[0, 0, 0, k]
        a, b = frac[0, 0, 0, 0, k], frac[0, 0, 0, 1, k]
        to_first = owner[0, 0, 0, k] == 0
        mixed = (1.0 - a) * out_ref[row] + a * out_ref[row + 1]
        here = (256 + to - col) & 127
        beyond = (255 + to - col) & 127
        value = (1.0 - b) * pltpu.roll(mixed, here, 1) + b * pltpu.roll(mixed, beyond, 1)
        to = jnp.where(k < live, to, 128)
        first = jnp.where(wide == jnp.where(to_first, to, 128), value, first)
        last = jnp.where(wide == jnp.where(to_first, 128, to), value, last)
        return first, last

    zero = jnp.zeros((channels, 128), jnp.float32)
    first, last = lax.fori_loop(0, slots, donate, (zero, zero), unroll=8)
    rim_out[0] = first
    rim_out[1] = last

    sends = []
    for n, m in enumerate((0, lon_count - 1)):
        copy = pltpu.make_async_remote_copy(
            src_ref=rim_out.at[n], dst_ref=rim_in.at[i], send_sem=rim_send.at[n],
            recv_sem=rim_recv.at[i], device_id=(1 - p, m, j), device_id_type=MESH,
        )
        copy.start()
        sends.append(copy)

    @pl.when(is_rim)
    def _():
        total = zero
        for m in range(lon_count):
            pltpu.make_async_remote_copy(
                src_ref=rim_out.at[0], dst_ref=rim_in.at[m], send_sem=rim_send.at[0],
                recv_sem=rim_recv.at[m], device_id=(1 - p, m, j), device_id_type=MESH,
            ).wait_recv()
            total = total + rim_in[m]
        out_ref[jnp.where(i == 0, 0, rows - 1)] = total

    for copy, there, _ in copies:
        pl.when(there)(copy.wait_send)
    for copy in sends:
        copy.wait_send()


def body(fields, offsets, fractions, send_count, send_owner, send_cell, send_target, send_frac):
    _, channels, rows, columns = fields.shape
    lon_count, lat_count = lax.axis_size("lon"), lax.axis_size("lat")
    slots = send_owner.shape[-1]
    groups = rows // PER
    hbm = pl.BlockSpec(memory_space=pltpu.HBM)
    vmem = pl.BlockSpec(memory_space=pltpu.VMEM)
    f32 = jnp.float32
    out = pl.pallas_call(
        functools.partial(kernel, lon_count, lat_count, rows, channels, slots),
        out_shape=jax.ShapeDtypeStruct((rows, channels, columns), f32),
        in_specs=[hbm, pl.BlockSpec(memory_space=pltpu.SMEM)] + [hbm] * 6,
        out_specs=vmem,
        scratch_shapes=[
            pltpu.SMEM((2, 1, rows // TILE), jnp.int32),
            pltpu.SMEM(send_owner.shape, jnp.int32),
            pltpu.SMEM(send_cell.shape, jnp.int32),
            pltpu.SMEM(send_target.shape, jnp.int32),
            pltpu.SMEM(send_frac.shape, f32),
            pltpu.VMEM((channels * rows, columns), f32),
            pltpu.VMEM((2, rows, columns), f32),
            pltpu.VMEM((LOW + rows + HIGH, channels, columns), f32),
            pltpu.VMEM((LOW, channels, columns), f32),
            pltpu.VMEM((HIGH, channels, columns), f32),
            pltpu.VMEM((groups, channels, columns), f32),
            pltpu.VMEM((groups, channels, columns), f32),
            pltpu.VMEM((groups + 3, channels, columns), f32),
            pltpu.VMEM((groups + 3, channels, columns), f32),
            pltpu.VMEM((LOW + rows + HIGH, channels, columns), f32),
            pltpu.VMEM((8, rows, columns), f32),
            pltpu.VMEM((2, channels, columns), f32),
            pltpu.VMEM((lon_count, channels, columns), f32),
            pltpu.SemaphoreType.DMA((7,)),
            pltpu.SemaphoreType.DMA((9,)),
            pltpu.SemaphoreType.DMA((9,)),
            pltpu.SemaphoreType.DMA((2,)),
            pltpu.SemaphoreType.DMA((lon_count,)),
        ],
        compiler_params=pltpu.CompilerParams(
            collective_id=0, has_side_effects=True, vmem_limit_bytes=60 * 1024 * 1024
        ),
    )(
        offsets.reshape(2, 1, rows // TILE), send_count, send_owner, send_cell, send_target, send_frac,
        fields.reshape(channels * rows, columns), fractions.reshape(2, rows, columns),
    )
    return out.transpose(1, 0, 2)[None]


def solution(mesh):
    placed = (
        P("panel", None, "lon", "lat"),
        P("panel", None, "lon", "lat"),
        P("panel", None, "lon", "lat"),
        P("panel", "lon", "lat"),
        P("panel", "lon", "lat", None),
        P("panel", "lon", "lat", None),
        P("panel", "lon", "lat", None),
        P("panel", "lon", "lat", None, None),
    )
    return jax.shard_map(
        body, mesh=mesh, in_specs=placed, out_specs=P("panel", None, "lon", "lat"), check_vma=False
    )
```

```python
import functools

import jax
import jax.numpy as jnp
from jax import lax
from jax.experimental import pallas as pl
from jax.experimental.pallas import tpu as pltpu
from jax.sharding import PartitionSpec as P

TILE = 8
LOW = 8
HIGH = 9
STRIP = 16
PER = 128 // STRIP
MESH = pl.DeviceIdType.MESH


def lagrange(x):
    return (
        -x * (x - 1.0) * (x - 2.0) * (1.0 / 6.0),
        (x + 1.0) * (x - 1.0) * (x - 2.0) * 0.5,
        -(x + 1.0) * x * (x - 2.0) * 0.5,
        (x + 1.0) * x * (x - 1.0) * (1.0 / 6.0),
    )


def kernel(
    lon_count, lat_count, rows, channels, slots,
    offsets_hbm, count, owner_hbm, cell_hbm, target_hbm, frac_hbm, x_hbm, tall_hbm, fractions_hbm, out_ref,
    offsets, owner, cell, target, frac, x_ref, frac_ref,
    ext, adv, land_lo, land_hi, land_one, pack_l, pack_r, from_r, from_l, halo, weights, rim_out, rim_in,
    in_sem, send_sem, recv_sem, rim_send, rim_recv,
):
    p = lax.axis_index("panel")
    i = lax.axis_index("lon")
    j = lax.axis_index("lat")
    groups = rows // PER
    blocks = channels // 8
    own = LOW
    has_prev, has_next = i > 0, i < lon_count - 1
    has_left, has_right = j > 0, j < lat_count - 1
    is_rim = jnp.logical_or(i == 0, i == lon_count - 1)

    around = [
        (-1, 0, has_prev), (1, 0, has_next), (0, -1, has_left), (0, 1, has_right),
        (-1, -1, has_prev & has_left), (1, -1, has_next & has_left),
        (-1, 1, has_prev & has_right), (1, 1, has_next & has_right),
    ]
    barrier = pltpu.get_barrier_semaphore()
    waits = jnp.int32(0)
    for di, dj, there in around:
        @pl.when(there)
        def _(di=di, dj=dj):
            pl.semaphore_signal(barrier, inc=1, device_id=(p, i + di, j + dj), device_id_type=MESH)
        waits = waits + there.astype(jnp.int32)

    @pl.when(is_rim)
    def _():
        def greet(m, carry):
            pl.semaphore_signal(barrier, inc=1, device_id=(1 - p, m, j), device_id_type=MESH)
            return carry
        lax.fori_loop(0, lon_count, greet, 0)

    @pl.when(jnp.logical_not(is_rim))
    def _():
        for m in (0, lon_count - 1):
            pl.semaphore_signal(barrier, inc=1, device_id=(1 - p, m, j), device_id_type=MESH)

    waits = waits + jnp.where(is_rim, lon_count, 2)

    loads = [
        pltpu.make_async_copy(src, dst, in_sem.at[n])
        for n, (src, dst) in enumerate([
            (tall_hbm, x_ref), (fractions_hbm, frac_ref), (offsets_hbm, offsets),
            (owner_hbm, owner), (cell_hbm, cell), (target_hbm, target), (frac_hbm, frac),
        ])
    ]
    for load in loads:
        load.start()

    def clear(ref, start, size):
        ref[pl.ds(start, size)] = jnp.zeros((size,) + ref.shape[1:], jnp.float32)

    @pl.when(jnp.logical_not(has_prev))
    def _():
        clear(land_lo, 0, blocks)
        clear(from_r, 0, 1)
        clear(from_l, 0, 1)

    @pl.when(jnp.logical_not(has_next))
    def _():
        clear(land_hi, 0, blocks)
        clear(land_one, 0, blocks)
        clear(from_r, 1 + groups, 2)
        clear(from_l, 1 + groups, 2)

    @pl.when(jnp.logical_not(has_right))
    def _():
        clear(from_r, 0, groups + 3)

    @pl.when(jnp.logical_not(has_left))
    def _():
        clear(from_l, 0, groups + 3)

    lane = lax.broadcasted_iota(jnp.int32, (8, 128), 1)
    strip = lane // STRIP

    def pack(g):
        for c in range(blocks):
            left = jnp.zeros((8, 128), jnp.float32)
            right = jnp.zeros((8, 128), jnp.float32)
            for m in range(PER):
                row = g * PER + m
                v = x_ref[pl.ds(c * 8 * rows + row, 8, stride=rows), :]
                ext[c, own + row] = v
                rolled = pltpu.roll(v, STRIP * m, 1) if m else v
                left = jnp.where(strip == m, rolled, left)
                right = jnp.where(strip == (m + PER - 1) % PER, rolled, right)
            pack_l[g, pl.ds(c * 8, 8), :] = left
            pack_r[g, pl.ds(c * 8, 8), :] = right

    copies = []

    def send(src, dst, side):
        di, dj, there = around[side]
        n = len(copies)
        copy = pltpu.make_async_remote_copy(
            src_ref=src, dst_ref=dst, send_sem=send_sem.at[n], recv_sem=recv_sem.at[n],
            device_id=(p, i + di, j + dj), device_id_type=MESH,
        )
        arrives = [t for a, b, t in around if (a, b) == (-di, -dj)][0]
        copies.append((copy, there, arrives))
        pl.when(there)(copy.start)

    def arrive(n):
        copy, _, arrives = copies[n]
        pl.when(arrives)(copy.wait_recv)

    pl.semaphore_wait(barrier, waits)
    for c in range(blocks):
        part = pl.ds(c * 8, 8)
        send(x_hbm.at[part, pl.ds(0, 8), :], land_hi.at[c], 0)
        send(x_hbm.at[part, pl.ds(rows - LOW, LOW), :], land_lo.at[c], 1)
    loads[0].wait()
    for g in range(groups):
        pack(g)
    send(pack_l, from_r.at[pl.ds(1, groups)], 2)
    send(pack_r, from_l.at[pl.ds(1, groups)], 3)
    send(pack_l.at[pl.ds(0, 2)], from_r.at[pl.ds(1 + groups, 2)], 4)
    send(pack_l.at[pl.ds(groups - 1, 1)], from_r.at[pl.ds(0, 1)], 5)
    send(pack_r.at[pl.ds(0, 2)], from_l.at[pl.ds(1 + groups, 2)], 6)
    send(pack_r.at[pl.ds(groups - 1, 1)], from_l.at[pl.ds(0, 1)], 7)
    send(ext.at[:, own + 8], land_one, 0)

    loads[1].wait()
    for g in range(groups):
        at = pl.ds(g * 8, 8)
        for axis in range(2):
            for n, w in enumerate(lagrange(frac_ref[axis, at, :])):
                weights[4 * axis + n, at, :] = w
    for load in loads[2:]:
        load.wait()

    def unpack(g, count):
        for c in range(blocks):
            at = pl.ds(c * 8, 8)
            for m in range(count):
                a, b = from_r[g, at, :], from_l[g, at, :]
                if m:
                    a = pltpu.roll(a, 128 - STRIP * m, 1)
                    b = pltpu.roll(b, 128 - STRIP * m, 1)
                halo[c, g * PER + m] = jnp.where(lane < 64, a, b)

    def tile(t, c):
        start = t * TILE + LOW - 1 + offsets[0, 0, t]
        shift = offsets[1, 0, t]
        inside, turn = [], []
        for b in range(4):
            k = shift + (b - 1)
            inside.append((lane >= k) & (lane < 128 + k))
            turn.append((256 - k) & 127)
        shifted = []
        for r in range(TILE):
            while len(shifted) < r + 4:
                main, edge = ext[c, start + len(shifted)], halo[c, start + len(shifted)]
                shifted.append(
                    [pltpu.roll(jnp.where(inside[b], main, edge), turn[b], 1) for b in range(4)]
                )
            row = t * TILE + r
            w = [jnp.broadcast_to(weights[n, pl.ds(row, 1), :], (8, 128)) for n in range(8)]
            total = None
            for a in range(4):
                inner = w[4] * shifted[r + a][0]
                for b in range(1, 4):
                    inner = inner + w[4 + b] * shifted[r + a][b]
                total = w[a] * inner if total is None else total + w[a] * inner
            adv[c, row] = total
            out_ref[pl.ds(c * 8 * rows + row, 8, stride=rows), :] = total

    live = count[0, 0, 0]

    def donate(c, k, carry):
        first, last = carry
        place = cell[0, 0, 0, k]
        row, col = place >> 7, place & 127
        to = target[0, 0, 0, k]
        a, b = frac[0, 0, 0, 0, k], frac[0, 0, 0, 1, k]
        to_first = owner[0, 0, 0, k] == 0
        mixed = (1.0 - a) * adv[c, row] + a * adv[c, row + 1]
        here = (256 + to - col) & 127
        beyond = (255 + to - col) & 127
        value = (1.0 - b) * pltpu.roll(mixed, here, 1) + b * pltpu.roll(mixed, beyond, 1)
        to = jnp.where(k < live, to, 128)
        first = jnp.where(lane == jnp.where(to_first, to, 128), value, first)
        last = jnp.where(lane == jnp.where(to_first, 128, to), value, last)
        return first, last

    tiles = rows // TILE
    lat, diagonal, one = 2 * blocks, 2 * blocks + 2, 2 * blocks + 6
    for n in (lat, lat + 1):
        arrive(n)
    for g in range(1, 1 + groups):
        unpack(g, PER)
    for c in range(blocks):
        for t in range(1, tiles - 2):
            tile(t, c)
    for n in range(diagonal, diagonal + 4):
        arrive(n)
    unpack(0, PER)
    unpack(1 + groups, PER)
    unpack(2 + groups, 1)
    zero = jnp.zeros((8, 128), jnp.float32)
    sends = []
    for c in range(blocks):
        arrive(2 * c)
        arrive(2 * c + 1)
        if c == 0:
            arrive(one)
        ext[c, pl.ds(0, LOW)] = jnp.swapaxes(land_lo[c], 0, 1)
        ext[c, pl.ds(own + rows, 8)] = jnp.swapaxes(land_hi[c], 0, 1)
        ext[c, own + rows + 8] = land_one[c]
        for t in [0] + list(range(max(1, tiles - 2), tiles)):
            tile(t, c)
        first, last = lax.fori_loop(0, slots, functools.partial(donate, c), (zero, zero), unroll=8)
        rim_out[0, c] = first
        rim_out[1, c] = last
        for n, m in enumerate((0, lon_count - 1)):
            copy = pltpu.make_async_remote_copy(
                src_ref=rim_out.at[n, c], dst_ref=rim_in.at[i, c], send_sem=rim_send.at[n, c],
                recv_sem=rim_recv.at[i, c], device_id=(1 - p, m, j), device_id_type=MESH,
            )
            copy.start()
            sends.append(copy)

    @pl.when(is_rim)
    def _():
        rim_row = jnp.where(i == 0, 0, rows - 1)
        for c in range(blocks):
            total = zero
            for m in range(lon_count):
                pltpu.make_async_remote_copy(
                    src_ref=rim_out.at[0, c], dst_ref=rim_in.at[m, c], send_sem=rim_send.at[0, c],
                    recv_sem=rim_recv.at[m, c], device_id=(1 - p, m, j), device_id_type=MESH,
                ).wait_recv()
                total = total + rim_in[m, c]
            out_ref[pl.ds(c * 8 * rows + rim_row, 8, stride=rows), :] = total

    for copy, there, _ in copies:
        pl.when(there)(copy.wait_send)
    for copy in sends:
        copy.wait_send()


def body(fields, offsets, fractions, send_count, send_owner, send_cell, send_target, send_frac):
    _, channels, rows, columns = fields.shape
    lon_count, lat_count = lax.axis_size("lon"), lax.axis_size("lat")
    slots = send_owner.shape[-1]
    groups = rows // PER
    hbm = pl.BlockSpec(memory_space=pltpu.HBM)
    smem = pl.BlockSpec(memory_space=pltpu.SMEM)
    f32 = jnp.float32
    blocks = channels // 8
    reach = LOW + rows + HIGH
    operands = (
        offsets.reshape(2, 1, rows // TILE), send_owner, send_cell, send_target, send_frac,
        fields.reshape(channels, rows, columns), fields.reshape(channels * rows, columns),
        fractions.reshape(2, rows, columns),
    )
    operands = [pltpu.with_memory_space_constraint(x, pltpu.HBM) for x in operands]
    operands.insert(1, send_count)
    out = pl.pallas_call(
        functools.partial(kernel, lon_count, lat_count, rows, channels, slots),
        out_shape=jax.ShapeDtypeStruct((channels * rows, columns), f32),
        in_specs=[hbm, smem] + [hbm] * 7,
        out_specs=pl.BlockSpec(memory_space=pltpu.VMEM),
        scratch_shapes=[
            pltpu.SMEM((2, 1, rows // TILE), jnp.int32),
            pltpu.SMEM(send_owner.shape, jnp.int32),
            pltpu.SMEM(send_cell.shape, jnp.int32),
            pltpu.SMEM(send_target.shape, jnp.int32),
            pltpu.SMEM(send_frac.shape, f32),
            pltpu.VMEM((channels * rows, columns), f32),
            pltpu.VMEM((2, rows, columns), f32),
            pltpu.VMEM((blocks, reach, 8, columns), f32),
            pltpu.VMEM((blocks, rows, 8, columns), f32),
            pltpu.VMEM((blocks, 8, LOW, columns), f32),
            pltpu.VMEM((blocks, 8, 8, columns), f32),
            pltpu.VMEM((blocks, 8, columns), f32),
            pltpu.VMEM((groups, channels, columns), f32),
            pltpu.VMEM((groups, channels, columns), f32),
            pltpu.VMEM((groups + 3, channels, columns), f32),
            pltpu.VMEM((groups + 3, channels, columns), f32),
            pltpu.VMEM((blocks, reach, 8, columns), f32),
            pltpu.VMEM((8, rows, columns), f32),
            pltpu.VMEM((2, blocks, 8, columns), f32),
            pltpu.VMEM((lon_count, blocks, 8, columns), f32),
            pltpu.SemaphoreType.DMA((7,)),
            pltpu.SemaphoreType.DMA((2 * blocks + 7,)),
            pltpu.SemaphoreType.DMA((2 * blocks + 7,)),
            pltpu.SemaphoreType.DMA((2, blocks)),
            pltpu.SemaphoreType.DMA((lon_count, blocks)),
        ],
        compiler_params=pltpu.CompilerParams(
            collective_id=0, has_side_effects=True, vmem_limit_bytes=24 * 1024 * 1024
        ),
    )(*operands)
    return out.reshape(fields.shape)


def solution(mesh):
    placed = (
        P("panel", None, "lon", "lat"),
        P("panel", None, "lon", "lat"),
        P("panel", None, "lon", "lat"),
        P("panel", "lon", "lat"),
        P("panel", "lon", "lat", None),
        P("panel", "lon", "lat", None),
        P("panel", "lon", "lat", None),
        P("panel", "lon", "lat", None, None),
    )
    return jax.shard_map(
        body, mesh=mesh, in_specs=placed, out_specs=P("panel", None, "lon", "lat"), check_vma=False
    )
```

```python
import functools

import jax
import jax.numpy as jnp
from jax import lax
from jax.experimental import pallas as pl
from jax.experimental.pallas import tpu as pltpu
from jax.sharding import PartitionSpec as P

TILE = 8
LOW = 8
HIGH = 9
STRIP = 16
PER = 128 // STRIP
MESH = pl.DeviceIdType.MESH


def lagrange(x):
    return (
        -x * (x - 1.0) * (x - 2.0) * (1.0 / 6.0),
        (x + 1.0) * (x - 1.0) * (x - 2.0) * 0.5,
        -(x + 1.0) * x * (x - 2.0) * 0.5,
        (x + 1.0) * x * (x - 1.0) * (1.0 / 6.0),
    )


def kernel(
    lon_count, lat_count, rows, channels, slots,
    offsets_hbm, count, owner_hbm, cell_hbm, target_hbm, frac_hbm, x_hbm, tall_hbm, fractions_hbm, out_ref,
    offsets, owner, cell, target, frac, x_ref, frac_ref,
    ext, adv, land_lo, land_hi, land_one, pack_l, pack_r, from_r, from_l, halo, weights, slot_rows, rim_out, rim_in,
    in_sem, send_sem, recv_sem, rim_send, rim_recv,
):
    p = lax.axis_index("panel")
    i = lax.axis_index("lon")
    j = lax.axis_index("lat")
    groups = rows // PER
    blocks = channels // 8
    own = LOW
    has_prev, has_next = i > 0, i < lon_count - 1
    has_left, has_right = j > 0, j < lat_count - 1
    is_rim = jnp.logical_or(i == 0, i == lon_count - 1)

    around = [
        (-1, 0, has_prev), (1, 0, has_next), (0, -1, has_left), (0, 1, has_right),
        (-1, -1, has_prev & has_left), (1, -1, has_next & has_left),
        (-1, 1, has_prev & has_right), (1, 1, has_next & has_right),
    ]
    barrier = pltpu.get_barrier_semaphore()
    waits = jnp.int32(0)
    for di, dj, there in around:
        @pl.when(there)
        def _(di=di, dj=dj):
            pl.semaphore_signal(barrier, inc=1, device_id=(p, i + di, j + dj), device_id_type=MESH)
        waits = waits + there.astype(jnp.int32)

    @pl.when(is_rim)
    def _():
        def greet(m, carry):
            pl.semaphore_signal(barrier, inc=1, device_id=(1 - p, m, j), device_id_type=MESH)
            return carry
        lax.fori_loop(0, lon_count, greet, 0)

    @pl.when(jnp.logical_not(is_rim))
    def _():
        for m in (0, lon_count - 1):
            pl.semaphore_signal(barrier, inc=1, device_id=(1 - p, m, j), device_id_type=MESH)

    waits = waits + jnp.where(is_rim, lon_count, 2)

    loads = [
        pltpu.make_async_copy(src, dst, in_sem.at[n])
        for n, (src, dst) in enumerate([
            (tall_hbm, x_ref), (fractions_hbm, frac_ref), (offsets_hbm, offsets),
            (owner_hbm, owner), (cell_hbm, cell), (target_hbm, target), (frac_hbm, frac),
        ])
    ]
    for load in loads:
        load.start()

    def clear(ref, start, size):
        ref[pl.ds(start, size)] = jnp.zeros((size,) + ref.shape[1:], jnp.float32)

    @pl.when(jnp.logical_not(has_prev))
    def _():
        clear(land_lo, 0, blocks)
        clear(from_r, 0, 1)
        clear(from_l, 0, 1)

    @pl.when(jnp.logical_not(has_next))
    def _():
        clear(land_hi, 0, blocks)
        clear(land_one, 0, blocks)
        clear(from_r, 1 + groups, 2)
        clear(from_l, 1 + groups, 2)

    @pl.when(jnp.logical_not(has_right))
    def _():
        clear(from_r, 0, groups + 3)

    @pl.when(jnp.logical_not(has_left))
    def _():
        clear(from_l, 0, groups + 3)

    lane = lax.broadcasted_iota(jnp.int32, (8, 128), 1)
    strip = lane // STRIP

    def pack(g):
        for c in range(blocks):
            left = jnp.zeros((8, 128), jnp.float32)
            right = jnp.zeros((8, 128), jnp.float32)
            for m in range(PER):
                row = g * PER + m
                v = x_ref[pl.ds(c * 8 * rows + row, 8, stride=rows), :]
                ext[c, own + row] = v
                rolled = pltpu.roll(v, STRIP * m, 1) if m else v
                left = jnp.where(strip == m, rolled, left)
                right = jnp.where(strip == (m + PER - 1) % PER, rolled, right)
            pack_l[g, pl.ds(c * 8, 8), :] = left
            pack_r[g, pl.ds(c * 8, 8), :] = right

    copies = []

    def send(src, dst, side):
        di, dj, there = around[side]
        n = len(copies)
        copy = pltpu.make_async_remote_copy(
            src_ref=src, dst_ref=dst, send_sem=send_sem.at[n], recv_sem=recv_sem.at[n],
            device_id=(p, i + di, j + dj), device_id_type=MESH,
        )
        arrives = [t for a, b, t in around if (a, b) == (-di, -dj)][0]
        copies.append((copy, there, arrives))
        pl.when(there)(copy.start)

    def arrive(n):
        copy, _, arrives = copies[n]
        pl.when(arrives)(copy.wait_recv)

    pl.semaphore_wait(barrier, waits)
    for c in range(blocks):
        part = pl.ds(c * 8, 8)
        send(x_hbm.at[part, pl.ds(0, 8), :], land_hi.at[c], 0)
        send(x_hbm.at[part, pl.ds(rows - LOW, LOW), :], land_lo.at[c], 1)
    loads[0].wait()
    for g in range(groups):
        pack(g)
    send(pack_l, from_r.at[pl.ds(1, groups)], 2)
    send(pack_r, from_l.at[pl.ds(1, groups)], 3)
    send(pack_l.at[pl.ds(0, 2)], from_r.at[pl.ds(1 + groups, 2)], 4)
    send(pack_l.at[pl.ds(groups - 1, 1)], from_r.at[pl.ds(0, 1)], 5)
    send(pack_r.at[pl.ds(0, 2)], from_l.at[pl.ds(1 + groups, 2)], 6)
    send(pack_r.at[pl.ds(groups - 1, 1)], from_l.at[pl.ds(0, 1)], 7)
    send(ext.at[:, own + 8], land_one, 0)

    loads[1].wait()
    for g in range(groups):
        at = pl.ds(g * 8, 8)
        for axis in range(2):
            for n, w in enumerate(lagrange(frac_ref[axis, at, :])):
                weights[4 * axis + n, at, :] = w
    for load in loads[2:]:
        load.wait()

    live = count[0, 0, 0]
    line = lax.broadcasted_iota(jnp.int32, (1, 128), 1)

    def lay_out(k, carry):
        col = cell[0, 0, 0, k] & 127
        a, b = frac[0, 0, 0, 0, k], frac[0, 0, 0, 1, k]
        to = jnp.where(k < live, target[0, 0, 0, k], 128)
        to_first = owner[0, 0, 0, k] == 0
        across = jnp.where(line == col, 1.0 - b, jnp.where(line == col + 1, b, 0.0))
        at = pl.ds(k, 1)
        slot_rows[0, at, :] = (1.0 - a) * across
        slot_rows[1, at, :] = a * across
        slot_rows[2, at, :] = jnp.where(line == jnp.where(to_first, to, 128), 1.0, 0.0)
        slot_rows[3, at, :] = jnp.where(line == jnp.where(to_first, 128, to), 1.0, 0.0)
        return carry

    lax.fori_loop(0, slots, lay_out, 0, unroll=8)

    def unpack(g, count):
        for c in range(blocks):
            at = pl.ds(c * 8, 8)
            for m in range(count):
                a, b = from_r[g, at, :], from_l[g, at, :]
                if m:
                    a = pltpu.roll(a, 128 - STRIP * m, 1)
                    b = pltpu.roll(b, 128 - STRIP * m, 1)
                halo[c, g * PER + m] = jnp.where(lane < 64, a, b)

    def tile(t, c):
        start = t * TILE + LOW - 1 + offsets[0, 0, t]
        shift = offsets[1, 0, t]
        inside, turn = [], []
        for b in range(4):
            k = shift + (b - 1)
            inside.append((lane >= k) & (lane < 128 + k))
            turn.append((256 - k) & 127)
        shifted = []
        for r in range(TILE):
            while len(shifted) < r + 4:
                main, edge = ext[c, start + len(shifted)], halo[c, start + len(shifted)]
                shifted.append(
                    [pltpu.roll(jnp.where(inside[b], main, edge), turn[b], 1) for b in range(4)]
                )
            row = t * TILE + r
            w = [jnp.broadcast_to(weights[n, pl.ds(row, 1), :], (8, 128)) for n in range(8)]
            total = None
            for a in range(4):
                inner = w[4] * shifted[r + a][0]
                for b in range(1, 4):
                    inner = inner + w[4 + b] * shifted[r + a][b]
                total = w[a] * inner if total is None else total + w[a] * inner
            adv[c, row] = total
            out_ref[pl.ds(c * 8 * rows + row, 8, stride=rows), :] = total

    def donate(c, k, carry):
        first, last = carry
        row = cell[0, 0, 0, k] >> 7
        at = pl.ds(k, 1)
        mixed = slot_rows[0, at, :] * adv[c, row] + slot_rows[1, at, :] * adv[c, row + 1]
        value = jnp.sum(mixed, axis=1, keepdims=True)
        return first + slot_rows[2, at, :] * value, last + slot_rows[3, at, :] * value

    tiles = rows // TILE
    lat, diagonal, one = 2 * blocks, 2 * blocks + 2, 2 * blocks + 6
    for n in (lat, lat + 1):
        arrive(n)
    for g in range(1, 1 + groups):
        unpack(g, PER)
    for c in range(blocks):
        for t in range(1, tiles - 2):
            tile(t, c)
    for n in range(diagonal, diagonal + 4):
        arrive(n)
    unpack(0, PER)
    unpack(1 + groups, PER)
    unpack(2 + groups, 1)
    zero = jnp.zeros((8, 128), jnp.float32)
    sends = []
    for c in range(blocks):
        arrive(2 * c)
        arrive(2 * c + 1)
        if c == 0:
            arrive(one)
        ext[c, pl.ds(0, LOW)] = jnp.swapaxes(land_lo[c], 0, 1)
        ext[c, pl.ds(own + rows, 8)] = jnp.swapaxes(land_hi[c], 0, 1)
        ext[c, own + rows + 8] = land_one[c]
        for t in [0] + list(range(max(1, tiles - 2), tiles)):
            tile(t, c)
        first, last = lax.fori_loop(0, slots, functools.partial(donate, c), (zero, zero), unroll=8)
        rim_out[0, c] = first
        rim_out[1, c] = last
        for n, m in enumerate((0, lon_count - 1)):
            copy = pltpu.make_async_remote_copy(
                src_ref=rim_out.at[n, c], dst_ref=rim_in.at[i, c], send_sem=rim_send.at[n, c],
                recv_sem=rim_recv.at[i, c], device_id=(1 - p, m, j), device_id_type=MESH,
            )
            copy.start()
            sends.append(copy)

    @pl.when(is_rim)
    def _():
        rim_row = jnp.where(i == 0, 0, rows - 1)
        for c in range(blocks):
            total = zero
            for m in range(lon_count):
                pltpu.make_async_remote_copy(
                    src_ref=rim_out.at[0, c], dst_ref=rim_in.at[m, c], send_sem=rim_send.at[0, c],
                    recv_sem=rim_recv.at[m, c], device_id=(1 - p, m, j), device_id_type=MESH,
                ).wait_recv()
                total = total + rim_in[m, c]
            out_ref[pl.ds(c * 8 * rows + rim_row, 8, stride=rows), :] = total

    for copy, there, _ in copies:
        pl.when(there)(copy.wait_send)
    for copy in sends:
        copy.wait_send()


def body(fields, offsets, fractions, send_count, send_owner, send_cell, send_target, send_frac):
    _, channels, rows, columns = fields.shape
    lon_count, lat_count = lax.axis_size("lon"), lax.axis_size("lat")
    slots = send_owner.shape[-1]
    groups = rows // PER
    hbm = pl.BlockSpec(memory_space=pltpu.HBM)
    smem = pl.BlockSpec(memory_space=pltpu.SMEM)
    f32 = jnp.float32
    blocks = channels // 8
    reach = LOW + rows + HIGH
    operands = (
        offsets.reshape(2, 1, rows // TILE), send_owner, send_cell, send_target, send_frac,
        fields.reshape(channels, rows, columns), fields.reshape(channels * rows, columns),
        fractions.reshape(2, rows, columns),
    )
    operands = [pltpu.with_memory_space_constraint(x, pltpu.HBM) for x in operands]
    operands.insert(1, send_count)
    out = pl.pallas_call(
        functools.partial(kernel, lon_count, lat_count, rows, channels, slots),
        out_shape=jax.ShapeDtypeStruct((channels * rows, columns), f32),
        in_specs=[hbm, smem] + [hbm] * 7,
        out_specs=pl.BlockSpec(memory_space=pltpu.VMEM),
        scratch_shapes=[
            pltpu.SMEM((2, 1, rows // TILE), jnp.int32),
            pltpu.SMEM(send_owner.shape, jnp.int32),
            pltpu.SMEM(send_cell.shape, jnp.int32),
            pltpu.SMEM(send_target.shape, jnp.int32),
            pltpu.SMEM(send_frac.shape, f32),
            pltpu.VMEM((channels * rows, columns), f32),
            pltpu.VMEM((2, rows, columns), f32),
            pltpu.VMEM((blocks, reach, 8, columns), f32),
            pltpu.VMEM((blocks, rows, 8, columns), f32),
            pltpu.VMEM((blocks, 8, LOW, columns), f32),
            pltpu.VMEM((blocks, 8, 8, columns), f32),
            pltpu.VMEM((blocks, 8, columns), f32),
            pltpu.VMEM((groups, channels, columns), f32),
            pltpu.VMEM((groups, channels, columns), f32),
            pltpu.VMEM((groups + 3, channels, columns), f32),
            pltpu.VMEM((groups + 3, channels, columns), f32),
            pltpu.VMEM((blocks, reach, 8, columns), f32),
            pltpu.VMEM((8, rows, columns), f32),
            pltpu.VMEM((4, slots, columns), f32),
            pltpu.VMEM((2, blocks, 8, columns), f32),
            pltpu.VMEM((lon_count, blocks, 8, columns), f32),
            pltpu.SemaphoreType.DMA((7,)),
            pltpu.SemaphoreType.DMA((2 * blocks + 7,)),
            pltpu.SemaphoreType.DMA((2 * blocks + 7,)),
            pltpu.SemaphoreType.DMA((2, blocks)),
            pltpu.SemaphoreType.DMA((lon_count, blocks)),
        ],
        compiler_params=pltpu.CompilerParams(
            collective_id=0, has_side_effects=True, vmem_limit_bytes=24 * 1024 * 1024
        ),
    )(*operands)
    return out.reshape(fields.shape)


def solution(mesh):
    placed = (
        P("panel", None, "lon", "lat"),
        P("panel", None, "lon", "lat"),
        P("panel", None, "lon", "lat"),
        P("panel", "lon", "lat"),
        P("panel", "lon", "lat", None),
        P("panel", "lon", "lat", None),
        P("panel", "lon", "lat", None),
        P("panel", "lon", "lat", None, None),
    )
    return jax.shard_map(
        body, mesh=mesh, in_specs=placed, out_specs=P("panel", None, "lon", "lat"), check_vma=False
    )
```

```python
import functools

import jax
import jax.numpy as jnp
from jax import lax
from jax.experimental import pallas as pl
from jax.experimental.pallas import tpu as pltpu
from jax.sharding import PartitionSpec as P

TILE = 8
LOW = 8
HIGH = 9
STRIP = 16
PER = 128 // STRIP
MESH = pl.DeviceIdType.MESH


def lagrange(x):
    return (
        -x * (x - 1.0) * (x - 2.0) * (1.0 / 6.0),
        (x + 1.0) * (x - 1.0) * (x - 2.0) * 0.5,
        -(x + 1.0) * x * (x - 2.0) * 0.5,
        (x + 1.0) * x * (x - 1.0) * (1.0 / 6.0),
    )


def kernel(
    lon_count, lat_count, rows, channels, slots,
    offsets_hbm, count, owner_hbm, cell_hbm, target_hbm, frac_hbm, x_hbm, tall_hbm, fractions_hbm, out_ref,
    offsets, owner, cell, target, frac, x_ref, frac_ref,
    ext, adv, land_lo, land_hi, land_one, one_out, pack_l, pack_r, from_r, from_l, halo, weights, slot_rows, rim_out, rim_in,
    in_sem, send_sem, recv_sem, rim_send, rim_recv,
):
    p = lax.axis_index("panel")
    i = lax.axis_index("lon")
    j = lax.axis_index("lat")
    groups = rows // PER
    blocks = channels // 8
    own = LOW
    has_prev, has_next = i > 0, i < lon_count - 1
    has_left, has_right = j > 0, j < lat_count - 1
    is_rim = jnp.logical_or(i == 0, i == lon_count - 1)

    around = [
        (-1, 0, has_prev), (1, 0, has_next), (0, -1, has_left), (0, 1, has_right),
        (-1, -1, has_prev & has_left), (1, -1, has_next & has_left),
        (-1, 1, has_prev & has_right), (1, 1, has_next & has_right),
    ]
    barrier = pltpu.get_barrier_semaphore()
    waits = jnp.int32(0)
    for di, dj, there in around:
        @pl.when(there)
        def _(di=di, dj=dj):
            pl.semaphore_signal(barrier, inc=1, device_id=(p, i + di, j + dj), device_id_type=MESH)
        waits = waits + there.astype(jnp.int32)

    @pl.when(is_rim)
    def _():
        def greet(m, carry):
            pl.semaphore_signal(barrier, inc=1, device_id=(1 - p, m, j), device_id_type=MESH)
            return carry
        lax.fori_loop(0, lon_count, greet, 0)

    @pl.when(jnp.logical_not(is_rim))
    def _():
        for m in (0, lon_count - 1):
            pl.semaphore_signal(barrier, inc=1, device_id=(1 - p, m, j), device_id_type=MESH)

    waits = waits + jnp.where(is_rim, lon_count, 2)

    loads = [
        pltpu.make_async_copy(src, dst, in_sem.at[n])
        for n, (src, dst) in enumerate([
            (tall_hbm, x_ref), (fractions_hbm, frac_ref), (offsets_hbm, offsets),
            (owner_hbm, owner), (cell_hbm, cell), (target_hbm, target), (frac_hbm, frac),
        ])
    ]
    for load in loads:
        load.start()

    def clear(ref, start, size):
        ref[pl.ds(start, size)] = jnp.zeros((size,) + ref.shape[1:], jnp.float32)

    @pl.when(jnp.logical_not(has_prev))
    def _():
        clear(land_lo, 0, blocks)
        clear(from_r, 0, 1)
        clear(from_l, 0, 1)

    @pl.when(jnp.logical_not(has_next))
    def _():
        clear(land_hi, 0, blocks)
        clear(land_one, 0, blocks)
        clear(from_r, 1 + groups, 2)
        clear(from_l, 1 + groups, 2)

    @pl.when(jnp.logical_not(has_right))
    def _():
        clear(from_r, 0, groups + 3)

    @pl.when(jnp.logical_not(has_left))
    def _():
        clear(from_l, 0, groups + 3)

    lane = lax.broadcasted_iota(jnp.int32, (8, 128), 1)
    strip = lane // STRIP

    def pack(g):
        for c in range(blocks):
            left = jnp.zeros((8, 128), jnp.float32)
            right = jnp.zeros((8, 128), jnp.float32)
            for m in range(PER):
                row = g * PER + m
                v = x_ref[pl.ds(c * 8 * rows + row, 8, stride=rows), :]
                ext[c, own + row] = v
                rolled = pltpu.roll(v, STRIP * m, 1) if m else v
                left = jnp.where(strip == m, rolled, left)
                right = jnp.where(strip == (m + PER - 1) % PER, rolled, right)
            pack_l[g, pl.ds(c * 8, 8), :] = left
            pack_r[g, pl.ds(c * 8, 8), :] = right

    copies = []

    def send(src, dst, side):
        di, dj, there = around[side]
        n = len(copies)
        copy = pltpu.make_async_remote_copy(
            src_ref=src, dst_ref=dst, send_sem=send_sem.at[n], recv_sem=recv_sem.at[n],
            device_id=(p, i + di, j + dj), device_id_type=MESH,
        )
        arrives = [t for a, b, t in around if (a, b) == (-di, -dj)][0]
        copies.append((copy, there, arrives))
        pl.when(there)(copy.start)

    def arrive(n):
        copy, _, arrives = copies[n]
        pl.when(arrives)(copy.wait_recv)

    pl.semaphore_wait(barrier, waits)

    def send_tiles(c):
        part = pl.ds(c * 8, 8)
        send(x_hbm.at[part, pl.ds(0, 8), :], land_hi.at[c], 0)
        send(x_hbm.at[part, pl.ds(rows - LOW, LOW), :], land_lo.at[c], 1)

    send_tiles(0)
    loads[0].wait()
    for c in range(blocks):
        one_out[c] = x_ref[pl.ds(c * 8 * rows + 8, 8, stride=rows), :]
    send(one_out, land_one, 0)
    for c in range(1, blocks - 1):
        send_tiles(c)
    for g in range(groups):
        pack(g)
    send(pack_l, from_r.at[pl.ds(1, groups)], 2)
    send(pack_r, from_l.at[pl.ds(1, groups)], 3)
    send(pack_l.at[pl.ds(0, 2)], from_r.at[pl.ds(1 + groups, 2)], 4)
    send(pack_l.at[pl.ds(groups - 1, 1)], from_r.at[pl.ds(0, 1)], 5)
    send(pack_r.at[pl.ds(0, 2)], from_l.at[pl.ds(1 + groups, 2)], 6)
    send(pack_r.at[pl.ds(groups - 1, 1)], from_l.at[pl.ds(0, 1)], 7)
    send_tiles(blocks - 1)

    loads[1].wait()
    for g in range(groups):
        at = pl.ds(g * 8, 8)
        for axis in range(2):
            for n, w in enumerate(lagrange(frac_ref[axis, at, :])):
                weights[4 * axis + n, at, :] = w
    for load in loads[2:]:
        load.wait()

    live = count[0, 0, 0]
    line = lax.broadcasted_iota(jnp.int32, (1, 128), 1)

    def lay_out(k, carry):
        col = cell[0, 0, 0, k] & 127
        a, b = frac[0, 0, 0, 0, k], frac[0, 0, 0, 1, k]
        to = jnp.where(k < live, target[0, 0, 0, k], 128)
        to_first = owner[0, 0, 0, k] == 0
        across = jnp.where(line == col, 1.0 - b, jnp.where(line == col + 1, b, 0.0))
        at = pl.ds(k, 1)
        slot_rows[0, at, :] = (1.0 - a) * across
        slot_rows[1, at, :] = a * across
        slot_rows[2, at, :] = jnp.where(line == jnp.where(to_first, to, 128), 1.0, 0.0)
        slot_rows[3, at, :] = jnp.where(line == jnp.where(to_first, 128, to), 1.0, 0.0)
        return carry

    lax.fori_loop(0, slots, lay_out, 0, unroll=8)

    def unpack(g, count):
        for c in range(blocks):
            at = pl.ds(c * 8, 8)
            for m in range(count):
                a, b = from_r[g, at, :], from_l[g, at, :]
                if m:
                    a = pltpu.roll(a, 128 - STRIP * m, 1)
                    b = pltpu.roll(b, 128 - STRIP * m, 1)
                halo[c, g * PER + m] = jnp.where(lane < 64, a, b)

    def tile(t, c):
        start = t * TILE + LOW - 1 + offsets[0, 0, t]
        shift = offsets[1, 0, t]
        inside, turn = [], []
        for b in range(4):
            k = shift + (b - 1)
            inside.append((lane >= k) & (lane < 128 + k))
            turn.append((256 - k) & 127)
        shifted = []
        for r in range(TILE):
            while len(shifted) < r + 4:
                main, edge = ext[c, start + len(shifted)], halo[c, start + len(shifted)]
                shifted.append(
                    [pltpu.roll(jnp.where(inside[b], main, edge), turn[b], 1) for b in range(4)]
                )
            row = t * TILE + r
            w = [jnp.broadcast_to(weights[n, pl.ds(row, 1), :], (8, 128)) for n in range(8)]
            total = None
            for a in range(4):
                inner = w[4] * shifted[r + a][0]
                for b in range(1, 4):
                    inner = inner + w[4 + b] * shifted[r + a][b]
                total = w[a] * inner if total is None else total + w[a] * inner
            adv[c, row] = total
            out_ref[pl.ds(c * 8 * rows + row, 8, stride=rows), :] = total

    def donate(c, k, carry):
        first, last = carry
        row = cell[0, 0, 0, k] >> 7
        at = pl.ds(k, 1)
        mixed = slot_rows[0, at, :] * adv[c, row] + slot_rows[1, at, :] * adv[c, row + 1]
        value = jnp.sum(mixed, axis=1, keepdims=True)
        return first + slot_rows[2, at, :] * value, last + slot_rows[3, at, :] * value

    tiles = rows // TILE
    one, lat = 2, 2 * blocks + 1 - 2
    diagonal, last_tiles = lat + 2, lat + 6
    for n in (lat, lat + 1):
        arrive(n)
    for g in range(1, 1 + groups):
        unpack(g, PER)
    for c in range(blocks):
        for t in range(1, tiles - 2):
            tile(t, c)
    for n in range(diagonal, diagonal + 4):
        arrive(n)
    unpack(0, PER)
    unpack(1 + groups, PER)
    unpack(2 + groups, 1)
    zero = jnp.zeros((8, 128), jnp.float32)
    sends = []
    for c in range(blocks):
        at = 0 if c == 0 else last_tiles if c == blocks - 1 else 2 * c + 1
        arrive(at)
        arrive(at + 1)
        if c == 0:
            arrive(one)
        ext[c, pl.ds(0, LOW)] = jnp.swapaxes(land_lo[c], 0, 1)
        ext[c, pl.ds(own + rows, 8)] = jnp.swapaxes(land_hi[c], 0, 1)
        ext[c, own + rows + 8] = land_one[c]
        for t in [0] + list(range(max(1, tiles - 2), tiles)):
            tile(t, c)
        first, last = lax.fori_loop(0, slots, functools.partial(donate, c), (zero, zero), unroll=8)
        rim_out[0, c] = first
        rim_out[1, c] = last
        for n, m in enumerate((0, lon_count - 1)):
            copy = pltpu.make_async_remote_copy(
                src_ref=rim_out.at[n, c], dst_ref=rim_in.at[i, c], send_sem=rim_send.at[n, c],
                recv_sem=rim_recv.at[i, c], device_id=(1 - p, m, j), device_id_type=MESH,
            )
            copy.start()
            sends.append(copy)

    @pl.when(is_rim)
    def _():
        rim_row = jnp.where(i == 0, 0, rows - 1)
        for c in range(blocks):
            total = zero
            for m in range(lon_count):
                pltpu.make_async_remote_copy(
                    src_ref=rim_out.at[0, c], dst_ref=rim_in.at[m, c], send_sem=rim_send.at[0, c],
                    recv_sem=rim_recv.at[m, c], device_id=(1 - p, m, j), device_id_type=MESH,
                ).wait_recv()
                total = total + rim_in[m, c]
            out_ref[pl.ds(c * 8 * rows + rim_row, 8, stride=rows), :] = total

    for copy, there, _ in copies:
        pl.when(there)(copy.wait_send)
    for copy in sends:
        copy.wait_send()


def body(fields, offsets, fractions, send_count, send_owner, send_cell, send_target, send_frac):
    _, channels, rows, columns = fields.shape
    lon_count, lat_count = lax.axis_size("lon"), lax.axis_size("lat")
    slots = send_owner.shape[-1]
    groups = rows // PER
    hbm = pl.BlockSpec(memory_space=pltpu.HBM)
    smem = pl.BlockSpec(memory_space=pltpu.SMEM)
    f32 = jnp.float32
    blocks = channels // 8
    reach = LOW + rows + HIGH
    operands = (
        offsets.reshape(2, 1, rows // TILE), send_owner, send_cell, send_target, send_frac,
        fields.reshape(channels, rows, columns), fields.reshape(channels * rows, columns),
        fractions.reshape(2, rows, columns),
    )
    operands = [pltpu.with_memory_space_constraint(x, pltpu.HBM) for x in operands]
    operands.insert(1, send_count)
    out = pl.pallas_call(
        functools.partial(kernel, lon_count, lat_count, rows, channels, slots),
        out_shape=jax.ShapeDtypeStruct((channels * rows, columns), f32),
        in_specs=[hbm, smem] + [hbm] * 7,
        out_specs=pl.BlockSpec(memory_space=pltpu.VMEM),
        scratch_shapes=[
            pltpu.SMEM((2, 1, rows // TILE), jnp.int32),
            pltpu.SMEM(send_owner.shape, jnp.int32),
            pltpu.SMEM(send_cell.shape, jnp.int32),
            pltpu.SMEM(send_target.shape, jnp.int32),
            pltpu.SMEM(send_frac.shape, f32),
            pltpu.VMEM((channels * rows, columns), f32),
            pltpu.VMEM((2, rows, columns), f32),
            pltpu.VMEM((blocks, reach, 8, columns), f32),
            pltpu.VMEM((blocks, rows, 8, columns), f32),
            pltpu.VMEM((blocks, 8, LOW, columns), f32),
            pltpu.VMEM((blocks, 8, 8, columns), f32),
            pltpu.VMEM((blocks, 8, columns), f32),
            pltpu.VMEM((blocks, 8, columns), f32),
            pltpu.VMEM((groups, channels, columns), f32),
            pltpu.VMEM((groups, channels, columns), f32),
            pltpu.VMEM((groups + 3, channels, columns), f32),
            pltpu.VMEM((groups + 3, channels, columns), f32),
            pltpu.VMEM((blocks, reach, 8, columns), f32),
            pltpu.VMEM((8, rows, columns), f32),
            pltpu.VMEM((4, slots, columns), f32),
            pltpu.VMEM((2, blocks, 8, columns), f32),
            pltpu.VMEM((lon_count, blocks, 8, columns), f32),
            pltpu.SemaphoreType.DMA((7,)),
            pltpu.SemaphoreType.DMA((2 * blocks + 7,)),
            pltpu.SemaphoreType.DMA((2 * blocks + 7,)),
            pltpu.SemaphoreType.DMA((2, blocks)),
            pltpu.SemaphoreType.DMA((lon_count, blocks)),
        ],
        compiler_params=pltpu.CompilerParams(
            collective_id=0, has_side_effects=True, vmem_limit_bytes=24 * 1024 * 1024
        ),
    )(*operands)
    return out.reshape(fields.shape)


def solution(mesh):
    placed = (
        P("panel", None, "lon", "lat"),
        P("panel", None, "lon", "lat"),
        P("panel", None, "lon", "lat"),
        P("panel", "lon", "lat"),
        P("panel", "lon", "lat", None),
        P("panel", "lon", "lat", None),
        P("panel", "lon", "lat", None),
        P("panel", "lon", "lat", None, None),
    )
    return jax.shard_map(
        body, mesh=mesh, in_specs=placed, out_specs=P("panel", None, "lon", "lat"), check_vma=False
    )
```

```python
import functools

import jax
import jax.numpy as jnp
from jax import lax
from jax.experimental import pallas as pl
from jax.experimental.pallas import tpu as pltpu
from jax.sharding import PartitionSpec as P

TILE = 8
LOW = 8
HIGH = 9
STRIP = 16
PER = 128 // STRIP
MESH = pl.DeviceIdType.MESH


def lagrange(x):
    return (
        -x * (x - 1.0) * (x - 2.0) * (1.0 / 6.0),
        (x + 1.0) * (x - 1.0) * (x - 2.0) * 0.5,
        -(x + 1.0) * x * (x - 2.0) * 0.5,
        (x + 1.0) * x * (x - 1.0) * (1.0 / 6.0),
    )


def kernel(
    lon_count, lat_count, rows, channels, slots,
    offsets_hbm, count, owner_hbm, cell_hbm, target_hbm, frac_hbm, x_hbm, tall_hbm, fractions_hbm, out_ref,
    offsets, owner, cell, target, frac, x_ref, frac_ref,
    ext, adv, land_lo, land_hi, land_one, one_out, pack_l, pack_r, from_r, from_l, halo, weights, slot_rows, rim_out, rim_in,
    in_sem, send_sem, recv_sem, rim_send, rim_recv,
):
    p = lax.axis_index("panel")
    i = lax.axis_index("lon")
    j = lax.axis_index("lat")
    groups = rows // PER
    blocks = channels // 8
    own = LOW
    has_prev, has_next = i > 0, i < lon_count - 1
    has_left, has_right = j > 0, j < lat_count - 1
    is_rim = jnp.logical_or(i == 0, i == lon_count - 1)

    around = [
        (-1, 0, has_prev), (1, 0, has_next), (0, -1, has_left), (0, 1, has_right),
        (-1, -1, has_prev & has_left), (1, -1, has_next & has_left),
        (-1, 1, has_prev & has_right), (1, 1, has_next & has_right),
    ]
    barrier = pltpu.get_barrier_semaphore()
    waits = jnp.int32(0)
    for di, dj, there in around:
        @pl.when(there)
        def _(di=di, dj=dj):
            pl.semaphore_signal(barrier, inc=1, device_id=(p, i + di, j + dj), device_id_type=MESH)
        waits = waits + there.astype(jnp.int32)

    @pl.when(is_rim)
    def _():
        def greet(m, carry):
            pl.semaphore_signal(barrier, inc=1, device_id=(1 - p, m, j), device_id_type=MESH)
            return carry
        lax.fori_loop(0, lon_count, greet, 0)

    @pl.when(jnp.logical_not(is_rim))
    def _():
        for m in (0, lon_count - 1):
            pl.semaphore_signal(barrier, inc=1, device_id=(1 - p, m, j), device_id_type=MESH)

    waits = waits + jnp.where(is_rim, lon_count, 2)

    loads = [
        pltpu.make_async_copy(src, dst, in_sem.at[n])
        for n, (src, dst) in enumerate([
            (tall_hbm, x_ref), (fractions_hbm, frac_ref), (offsets_hbm, offsets),
            (owner_hbm, owner), (cell_hbm, cell), (target_hbm, target), (frac_hbm, frac),
        ])
    ]
    for load in loads:
        load.start()

    def clear(ref, start, size):
        ref[pl.ds(start, size)] = jnp.zeros((size,) + ref.shape[1:], jnp.float32)

    @pl.when(jnp.logical_not(has_prev))
    def _():
        clear(land_lo, 0, blocks)
        clear(from_r, 0, 1)
        clear(from_l, 0, 1)

    @pl.when(jnp.logical_not(has_next))
    def _():
        clear(land_hi, 0, blocks)
        clear(land_one, 0, blocks)
        clear(from_r, 1 + groups, 2)
        clear(from_l, 1 + groups, 2)

    @pl.when(jnp.logical_not(has_right))
    def _():
        clear(from_r, 0, groups + 3)

    @pl.when(jnp.logical_not(has_left))
    def _():
        clear(from_l, 0, groups + 3)

    lane = lax.broadcasted_iota(jnp.int32, (8, 128), 1)
    strip = lane // STRIP

    def pack(n, carry):
        g, c = n // blocks, n % blocks
        left = jnp.zeros((8, 128), jnp.float32)
        right = jnp.zeros((8, 128), jnp.float32)
        for m in range(PER):
            row = g * PER + m
            v = x_ref[pl.ds(c * (8 * rows) + row, 8, stride=rows), :]
            ext[c, own + row] = v
            rolled = pltpu.roll(v, STRIP * m, 1) if m else v
            left = jnp.where(strip == m, rolled, left)
            right = jnp.where(strip == (m + PER - 1) % PER, rolled, right)
        pack_l[g, c] = left
        pack_r[g, c] = right
        return carry

    copies = []

    def remote(src, dst, side, n):
        di, dj, there = around[side]
        copy = pltpu.make_async_remote_copy(
            src_ref=src, dst_ref=dst, send_sem=send_sem.at[n], recv_sem=recv_sem.at[n],
            device_id=(p, i + di, j + dj), device_id_type=MESH,
        )
        arrives = [t for a, b, t in around if (a, b) == (-di, -dj)][0]
        return copy, there, arrives

    def send(copy):
        copies.append(copy)
        pl.when(copy[1])(copy[0].start)

    def arrive(copy):
        pl.when(copy[2])(copy[0].wait_recv)

    def edge_tiles(c):
        part = pl.ds(pl.multiple_of(c * 8, 8), 8)
        return (
            remote(x_hbm.at[part, pl.ds(0, 8), :], land_hi.at[c], 0, 2 * c),
            remote(x_hbm.at[part, pl.ds(rows - LOW, LOW), :], land_lo.at[c], 1, 2 * c + 1),
        )

    pl.semaphore_wait(barrier, waits)

    for copy in edge_tiles(0):
        send(copy)
    loads[0].wait()
    for c in range(blocks):
        one_out[c] = x_ref[pl.ds(c * 8 * rows + 8, 8, stride=rows), :]
    base = 2 * blocks
    one = remote(one_out, land_one, 0, base)
    send(one)
    for c in range(1, blocks - 1):
        for copy in edge_tiles(c):
            send(copy)
    lax.fori_loop(0, groups * blocks, pack, 0)
    strips = [
        remote(pack_l, from_r.at[pl.ds(1, groups)], 2, base + 1),
        remote(pack_r, from_l.at[pl.ds(1, groups)], 3, base + 2),
        remote(pack_l.at[pl.ds(0, 2)], from_r.at[pl.ds(1 + groups, 2)], 4, base + 3),
        remote(pack_l.at[pl.ds(groups - 1, 1)], from_r.at[pl.ds(0, 1)], 5, base + 4),
        remote(pack_r.at[pl.ds(0, 2)], from_l.at[pl.ds(1 + groups, 2)], 6, base + 5),
        remote(pack_r.at[pl.ds(groups - 1, 1)], from_l.at[pl.ds(0, 1)], 7, base + 6),
    ]
    for copy in strips:
        send(copy)
    for copy in edge_tiles(blocks - 1):
        send(copy)

    loads[1].wait()

    def weigh(g, carry):
        at = pl.ds(pl.multiple_of(g * 8, 8), 8)
        for axis in range(2):
            for n, w in enumerate(lagrange(frac_ref[axis, at, :])):
                weights[4 * axis + n, at, :] = w
        return carry

    lax.fori_loop(0, groups, weigh, 0)
    for load in loads[2:]:
        load.wait()

    live = count[0, 0, 0]
    line = lax.broadcasted_iota(jnp.int32, (1, 128), 1)

    def lay_out(k, carry):
        col = cell[0, 0, 0, k] & 127
        a, b = frac[0, 0, 0, 0, k], frac[0, 0, 0, 1, k]
        to = jnp.where(k < live, target[0, 0, 0, k], 128)
        to_first = owner[0, 0, 0, k] == 0
        across = jnp.where(line == col, 1.0 - b, jnp.where(line == col + 1, b, 0.0))
        at = pl.ds(k, 1)
        slot_rows[0, at, :] = (1.0 - a) * across
        slot_rows[1, at, :] = a * across
        slot_rows[2, at, :] = jnp.where(line == jnp.where(to_first, to, 128), 1.0, 0.0)
        slot_rows[3, at, :] = jnp.where(line == jnp.where(to_first, 128, to), 1.0, 0.0)
        return carry

    lax.fori_loop(0, slots, lay_out, 0, unroll=4)

    def unpack(n, carry):
        g, c = n // blocks, n % blocks
        a, b = from_r[g, c], from_l[g, c]
        for m in range(PER):
            turned = [pltpu.roll(v, 128 - STRIP * m, 1) if m else v for v in (a, b)]
            halo[c, g * PER + m] = jnp.where(lane < 64, turned[0], turned[1])
        return carry

    def tile(t, c):
        start = t * TILE + LOW - 1 + offsets[0, 0, t]
        shift = offsets[1, 0, t]
        inside, turn = [], []
        for b in range(4):
            k = shift + (b - 1)
            inside.append((lane >= k) & (lane < 128 + k))
            turn.append((256 - k) & 127)
        shifted = []
        for r in range(TILE):
            while len(shifted) < r + 4:
                main, edge = ext[c, start + len(shifted)], halo[c, start + len(shifted)]
                shifted.append(
                    [pltpu.roll(jnp.where(inside[b], main, edge), turn[b], 1) for b in range(4)]
                )
            row = t * TILE + r
            w = [weights[n, pl.ds(row, 1), :] for n in range(8)]
            total = None
            for a in range(4):
                inner = w[4] * shifted[r + a][0]
                for b in range(1, 4):
                    inner = inner + w[4 + b] * shifted[r + a][b]
                total = w[a] * inner if total is None else total + w[a] * inner
            adv[c, row] = total
            out_ref[pl.ds(c * (8 * rows) + row, 8, stride=rows), :] = total

    def donate(c, k, carry):
        first, last = carry
        row = cell[0, 0, 0, k] >> 7
        at = pl.ds(k, 1)
        mixed = slot_rows[0, at, :] * adv[c, row] + slot_rows[1, at, :] * adv[c, row + 1]
        value = jnp.sum(mixed, axis=1, keepdims=True)
        return first + slot_rows[2, at, :] * value, last + slot_rows[3, at, :] * value

    tiles = rows // TILE
    for copy in strips:
        arrive(copy)
    lax.fori_loop(0, (groups + 3) * blocks, unpack, 0)
    first_inner, last_inner = 1, tiles - 2
    inner = max(last_inner - first_inner, 0)
    outer = tiles - inner

    def inner_tile(n, carry):
        tile(first_inner + n // blocks, n % blocks)
        return carry

    lax.fori_loop(0, inner * blocks, inner_tile, 0)
    arrive(one)
    zero = jnp.zeros((8, 128), jnp.float32)

    def rim_copies(c):
        return [
            pltpu.make_async_remote_copy(
                src_ref=rim_out.at[n, c], dst_ref=rim_in.at[i, c], send_sem=rim_send.at[n, c],
                recv_sem=rim_recv.at[i, c], device_id=(1 - p, m, j), device_id_type=MESH,
            )
            for n, m in enumerate((0, lon_count - 1))
        ]

    def finish_block(c, carry):
        for copy in edge_tiles(c):
            arrive(copy)
        ext[c, pl.ds(0, LOW)] = jnp.swapaxes(land_lo[c], 0, 1)
        ext[c, pl.ds(own + rows, 8)] = jnp.swapaxes(land_hi[c], 0, 1)
        ext[c, own + rows + 8] = land_one[c]

        def outer_tile(n, carry):
            tile(jnp.where(n < first_inner, n, n + inner), c)
            return carry

        lax.fori_loop(0, outer, outer_tile, 0)
        first, last = lax.fori_loop(0, slots, functools.partial(donate, c), (zero, zero), unroll=8)
        rim_out[0, c] = first
        rim_out[1, c] = last
        for copy in rim_copies(c):
            copy.start()
        return carry

    lax.fori_loop(0, blocks, finish_block, 0)

    @pl.when(is_rim)
    def _():
        rim_row = jnp.where(i == 0, 0, rows - 1)

        def collect(c, carry):
            total = zero
            for m in range(lon_count):
                pltpu.make_async_remote_copy(
                    src_ref=rim_out.at[0, c], dst_ref=rim_in.at[m, c], send_sem=rim_send.at[0, c],
                    recv_sem=rim_recv.at[m, c], device_id=(1 - p, m, j), device_id_type=MESH,
                ).wait_recv()
                total = total + rim_in[m, c]
            out_ref[pl.ds(c * (8 * rows) + rim_row, 8, stride=rows), :] = total
            return carry

        lax.fori_loop(0, blocks, collect, 0)

    for copy, there, _ in copies:
        pl.when(there)(copy.wait_send)
    for c in range(blocks):
        for copy in rim_copies(c):
            copy.wait_send()


def body(fields, offsets, fractions, send_count, send_owner, send_cell, send_target, send_frac):
    _, channels, rows, columns = fields.shape
    lon_count, lat_count = lax.axis_size("lon"), lax.axis_size("lat")
    slots = send_owner.shape[-1]
    groups = rows // PER
    hbm = pl.BlockSpec(memory_space=pltpu.HBM)
    smem = pl.BlockSpec(memory_space=pltpu.SMEM)
    f32 = jnp.float32
    blocks = channels // 8
    reach = LOW + rows + HIGH
    operands = (
        offsets.reshape(2, 1, rows // TILE), send_owner, send_cell, send_target, send_frac,
        fields.reshape(channels, rows, columns), fields.reshape(channels * rows, columns),
        fractions.reshape(2, rows, columns),
    )
    operands = [pltpu.with_memory_space_constraint(x, pltpu.HBM) for x in operands]
    operands.insert(1, send_count)
    out = pl.pallas_call(
        functools.partial(kernel, lon_count, lat_count, rows, channels, slots),
        out_shape=jax.ShapeDtypeStruct((channels * rows, columns), f32),
        in_specs=[hbm, smem] + [hbm] * 7,
        out_specs=pl.BlockSpec(memory_space=pltpu.VMEM),
        scratch_shapes=[
            pltpu.SMEM((2, 1, rows // TILE), jnp.int32),
            pltpu.SMEM(send_owner.shape, jnp.int32),
            pltpu.SMEM(send_cell.shape, jnp.int32),
            pltpu.SMEM(send_target.shape, jnp.int32),
            pltpu.SMEM(send_frac.shape, f32),
            pltpu.VMEM((channels * rows, columns), f32),
            pltpu.VMEM((2, rows, columns), f32),
            pltpu.VMEM((blocks, reach, 8, columns), f32),
            pltpu.VMEM((blocks, rows, 8, columns), f32),
            pltpu.VMEM((blocks, 8, LOW, columns), f32),
            pltpu.VMEM((blocks, 8, 8, columns), f32),
            pltpu.VMEM((blocks, 8, columns), f32),
            pltpu.VMEM((blocks, 8, columns), f32),
            pltpu.VMEM((groups, blocks, 8, columns), f32),
            pltpu.VMEM((groups, blocks, 8, columns), f32),
            pltpu.VMEM((groups + 3, blocks, 8, columns), f32),
            pltpu.VMEM((groups + 3, blocks, 8, columns), f32),
            pltpu.VMEM((blocks, (groups + 3) * PER, 8, columns), f32),
            pltpu.VMEM((8, rows, columns), f32),
            pltpu.VMEM((4, slots, columns), f32),
            pltpu.VMEM((2, blocks, 8, columns), f32),
            pltpu.VMEM((lon_count, blocks, 8, columns), f32),
            pltpu.SemaphoreType.DMA((7,)),
            pltpu.SemaphoreType.DMA((2 * blocks + 7,)),
            pltpu.SemaphoreType.DMA((2 * blocks + 7,)),
            pltpu.SemaphoreType.DMA((2, blocks)),
            pltpu.SemaphoreType.DMA((lon_count, blocks)),
        ],
        compiler_params=pltpu.CompilerParams(
            collective_id=0, has_side_effects=True, vmem_limit_bytes=24 * 1024 * 1024
        ),
    )(*operands)
    return out.reshape(fields.shape)


def solution(mesh):
    placed = (
        P("panel", None, "lon", "lat"),
        P("panel", None, "lon", "lat"),
        P("panel", None, "lon", "lat"),
        P("panel", "lon", "lat"),
        P("panel", "lon", "lat", None),
        P("panel", "lon", "lat", None),
        P("panel", "lon", "lat", None),
        P("panel", "lon", "lat", None, None),
    )
    return jax.shard_map(
        body, mesh=mesh, in_specs=placed, out_specs=P("panel", None, "lon", "lat"), check_vma=False
    )
```

```python
import functools

import jax
import jax.numpy as jnp
from jax import lax
from jax.experimental import pallas as pl
from jax.experimental.pallas import tpu as pltpu
from jax.sharding import PartitionSpec as P

TILE = 8
LOW = 8
HIGH = 9
STRIP = 16
PER = 128 // STRIP
MESH = pl.DeviceIdType.MESH


def lagrange(x):
    return (
        -x * (x - 1.0) * (x - 2.0) * (1.0 / 6.0),
        (x + 1.0) * (x - 1.0) * (x - 2.0) * 0.5,
        -(x + 1.0) * x * (x - 2.0) * 0.5,
        (x + 1.0) * x * (x - 1.0) * (1.0 / 6.0),
    )


def kernel(
    lon_count, lat_count, rows, channels, slots,
    offsets_hbm, count, owner_hbm, cell_hbm, target_hbm, frac_hbm, x_hbm, tall_hbm, fractions_hbm, out_ref,
    offsets, owner, cell, target, frac, x_ref, frac_ref,
    ext, adv, land_lo, land_hi, land_one, one_out, pack_l, pack_r, strips, halo, weights, slot_rows, rim_out, rim_in,
    in_sem, send_sem, recv_sem, rim_send, rim_recv,
):
    p = lax.axis_index("panel")
    i = lax.axis_index("lon")
    j = lax.axis_index("lat")
    groups = rows // PER
    blocks = channels // 8
    own = LOW
    from_r, from_l = strips.at[0], strips.at[1]
    has_prev, has_next = i > 0, i < lon_count - 1
    has_left, has_right = j > 0, j < lat_count - 1
    is_rim = jnp.logical_or(i == 0, i == lon_count - 1)

    around = [
        (-1, 0, has_prev), (1, 0, has_next), (0, -1, has_left), (0, 1, has_right),
        (-1, -1, has_prev & has_left), (1, -1, has_next & has_left),
        (-1, 1, has_prev & has_right), (1, 1, has_next & has_right),
    ]
    barrier = pltpu.get_barrier_semaphore()
    waits = jnp.int32(0)
    for di, dj, there in around:
        @pl.when(there)
        def _(di=di, dj=dj):
            pl.semaphore_signal(barrier, inc=1, device_id=(p, i + di, j + dj), device_id_type=MESH)
        waits = waits + there.astype(jnp.int32)

    @pl.when(is_rim)
    def _():
        def greet(m, carry):
            pl.semaphore_signal(barrier, inc=1, device_id=(1 - p, m, j), device_id_type=MESH)
            return carry
        lax.fori_loop(0, lon_count, greet, 0)

    @pl.when(jnp.logical_not(is_rim))
    def _():
        for m in (0, lon_count - 1):
            pl.semaphore_signal(barrier, inc=1, device_id=(1 - p, m, j), device_id_type=MESH)

    waits = waits + jnp.where(is_rim, lon_count, 2)

    loads = [
        pltpu.make_async_copy(src, dst, in_sem.at[n])
        for n, (src, dst) in enumerate([
            (tall_hbm, x_ref), (fractions_hbm, frac_ref), (offsets_hbm, offsets),
            (owner_hbm, owner), (cell_hbm, cell), (target_hbm, target), (frac_hbm, frac),
        ])
    ]
    for load in loads:
        load.start()

    def clear(ref, start, size):
        ref[pl.ds(start, size)] = jnp.zeros((size,) + ref.shape[1:], jnp.float32)

    @pl.when(jnp.logical_not(has_prev))
    def _():
        clear(land_lo, 0, blocks)
        clear(from_r, 0, 1)
        clear(from_l, 0, 1)

    @pl.when(jnp.logical_not(has_next))
    def _():
        clear(land_hi, 0, blocks)
        clear(land_one, 0, blocks)
        clear(from_r, 1 + groups, 2)
        clear(from_l, 1 + groups, 2)

    @pl.when(jnp.logical_not(has_right))
    def _():
        clear(from_r, 0, groups + 3)

    @pl.when(jnp.logical_not(has_left))
    def _():
        clear(from_l, 0, groups + 3)

    lane = lax.broadcasted_iota(jnp.int32, (8, 128), 1)
    strip = lane // STRIP

    def pack(g):
        for c in range(blocks):
            left = jnp.zeros((8, 128), jnp.float32)
            right = jnp.zeros((8, 128), jnp.float32)
            for m in range(PER):
                row = g * PER + m
                v = x_ref[pl.ds(c * 8 * rows + row, 8, stride=rows), :]
                ext[c, own + row] = v
                rolled = pltpu.roll(v, STRIP * m, 1) if m else v
                left = jnp.where(strip == m, rolled, left)
                right = jnp.where(strip == (m + PER - 1) % PER, rolled, right)
            pack_l[g, pl.ds(c * 8, 8), :] = left
            pack_r[g, pl.ds(c * 8, 8), :] = right

    copies = []

    def send(src, dst, side):
        di, dj, there = around[side]
        n = len(copies)
        copy = pltpu.make_async_remote_copy(
            src_ref=src, dst_ref=dst, send_sem=send_sem.at[n], recv_sem=recv_sem.at[n],
            device_id=(p, i + di, j + dj), device_id_type=MESH,
        )
        arrives = [t for a, b, t in around if (a, b) == (-di, -dj)][0]
        copies.append((copy, there, arrives))
        pl.when(there)(copy.start)

    def arrive(n):
        copy, _, arrives = copies[n]
        pl.when(arrives)(copy.wait_recv)

    pl.semaphore_wait(barrier, waits)

    def send_tiles(c):
        part = pl.ds(c * 8, 8)
        send(x_hbm.at[part, pl.ds(0, 8), :], land_hi.at[c], 0)
        send(x_hbm.at[part, pl.ds(rows - LOW, LOW), :], land_lo.at[c], 1)

    send_tiles(0)
    loads[0].wait()
    for c in range(blocks):
        one_out[c] = x_ref[pl.ds(c * 8 * rows + 8, 8, stride=rows), :]
    send(one_out, land_one, 0)
    for c in range(1, blocks - 1):
        send_tiles(c)
    for g in range(groups):
        pack(g)
    send(pack_l, from_r.at[pl.ds(1, groups)], 2)
    send(pack_r, from_l.at[pl.ds(1, groups)], 3)
    send(pack_l.at[pl.ds(0, 2)], from_r.at[pl.ds(1 + groups, 2)], 4)
    send(pack_l.at[pl.ds(groups - 1, 1)], from_r.at[pl.ds(0, 1)], 5)
    send(pack_r.at[pl.ds(0, 2)], from_l.at[pl.ds(1 + groups, 2)], 6)
    send(pack_r.at[pl.ds(groups - 1, 1)], from_l.at[pl.ds(0, 1)], 7)
    send_tiles(blocks - 1)

    loads[1].wait()
    for g in range(groups):
        at = pl.ds(g * 8, 8)
        for axis in range(2):
            for n, w in enumerate(lagrange(frac_ref[axis, at, :])):
                weights[4 * axis + n, at, :] = w
    for load in loads[2:]:
        load.wait()

    live = count[0, 0, 0]
    line = lax.broadcasted_iota(jnp.int32, (1, 128), 1)

    def lay_out(k, carry):
        col = cell[0, 0, 0, k] & 127
        a, b = frac[0, 0, 0, 0, k], frac[0, 0, 0, 1, k]
        to = jnp.where(k < live, target[0, 0, 0, k], 128)
        to_first = owner[0, 0, 0, k] == 0
        across = jnp.where(line == col, 1.0 - b, jnp.where(line == col + 1, b, 0.0))
        at = pl.ds(k, 1)
        slot_rows[0, at, :] = (1.0 - a) * across
        slot_rows[1, at, :] = a * across
        slot_rows[2, at, :] = jnp.where(line == jnp.where(to_first, to, 128), 1.0, 0.0)
        slot_rows[3, at, :] = jnp.where(line == jnp.where(to_first, 128, to), 1.0, 0.0)
        return carry

    lax.fori_loop(0, slots, lay_out, 0, unroll=8)

    side = jnp.where(has_right, 0, 1)
    kept = (lane < 64) == has_right

    def unpack(g, count):
        for c in range(blocks):
            at = pl.ds(c * 8, 8)
            for m in range(count):
                def turned(s):
                    v = strips[s, g, at, :]
                    return pltpu.roll(v, 128 - STRIP * m, 1) if m else v
                if lat_count == 2:
                    row = jnp.where(kept, turned(side), 0.0)
                else:
                    row = jnp.where(lane < 64, turned(0), turned(1))
                halo[c, g * PER + m] = row

    def tile(t, c):
        start = t * TILE + LOW - 1 + offsets[0, 0, t]
        shift = offsets[1, 0, t]
        inside, turn = [], []
        for b in range(4):
            k = shift + (b - 1)
            inside.append((lane >= k) & (lane < 128 + k))
            turn.append((256 - k) & 127)
        shifted = []
        for r in range(TILE):
            while len(shifted) < r + 4:
                main, edge = ext[c, start + len(shifted)], halo[c, start + len(shifted)]
                shifted.append(
                    [pltpu.roll(jnp.where(inside[b], main, edge), turn[b], 1) for b in range(4)]
                )
            row = t * TILE + r
            w = [jnp.broadcast_to(weights[n, pl.ds(row, 1), :], (8, 128)) for n in range(8)]
            total = None
            for a in range(4):
                inner = w[4] * shifted[r + a][0]
                for b in range(1, 4):
                    inner = inner + w[4 + b] * shifted[r + a][b]
                total = w[a] * inner if total is None else total + w[a] * inner
            adv[c, row] = total
            out_ref[pl.ds(c * 8 * rows + row, 8, stride=rows), :] = total

    def donate(c, k, carry):
        first, last = carry
        row = cell[0, 0, 0, k] >> 7
        at = pl.ds(k, 1)
        mixed = slot_rows[0, at, :] * adv[c, row] + slot_rows[1, at, :] * adv[c, row + 1]
        value = jnp.sum(mixed, axis=1, keepdims=True)
        return first + slot_rows[2, at, :] * value, last + slot_rows[3, at, :] * value

    tiles = rows // TILE
    one, lat = 2, 2 * blocks + 1 - 2
    diagonal, last_tiles = lat + 2, lat + 6
    for n in (lat, lat + 1):
        arrive(n)
    for g in range(1, 1 + groups):
        unpack(g, PER)
    for c in range(blocks):
        for t in range(1, tiles - 2):
            tile(t, c)
    for n in range(diagonal, diagonal + 4):
        arrive(n)
    unpack(0, PER)
    unpack(1 + groups, PER)
    unpack(2 + groups, 1)
    zero = jnp.zeros((8, 128), jnp.float32)
    sends = []
    for c in range(blocks):
        at = 0 if c == 0 else last_tiles if c == blocks - 1 else 2 * c + 1
        arrive(at)
        arrive(at + 1)
        if c == 0:
            arrive(one)
        ext[c, pl.ds(0, LOW)] = jnp.swapaxes(land_lo[c], 0, 1)
        ext[c, pl.ds(own + rows, 8)] = jnp.swapaxes(land_hi[c], 0, 1)
        ext[c, own + rows + 8] = land_one[c]
        for t in [0] + list(range(max(1, tiles - 2), tiles)):
            tile(t, c)
        first, last = lax.fori_loop(0, slots, functools.partial(donate, c), (zero, zero), unroll=slots)
        rim_out[0, c] = first
        rim_out[1, c] = last
        for n, m in enumerate((0, lon_count - 1)):
            copy = pltpu.make_async_remote_copy(
                src_ref=rim_out.at[n, c], dst_ref=rim_in.at[i, c], send_sem=rim_send.at[n, c],
                recv_sem=rim_recv.at[i, c], device_id=(1 - p, m, j), device_id_type=MESH,
            )
            copy.start()
            sends.append(copy)

    @pl.when(is_rim)
    def _():
        rim_row = jnp.where(i == 0, 0, rows - 1)
        for c in range(blocks):
            total = zero
            for m in range(lon_count):
                pltpu.make_async_remote_copy(
                    src_ref=rim_out.at[0, c], dst_ref=rim_in.at[m, c], send_sem=rim_send.at[0, c],
                    recv_sem=rim_recv.at[m, c], device_id=(1 - p, m, j), device_id_type=MESH,
                ).wait_recv()
                total = total + rim_in[m, c]
            out_ref[pl.ds(c * 8 * rows + rim_row, 8, stride=rows), :] = total

    for copy, there, _ in copies:
        pl.when(there)(copy.wait_send)
    for copy in sends:
        copy.wait_send()


def body(fields, offsets, fractions, send_count, send_owner, send_cell, send_target, send_frac):
    _, channels, rows, columns = fields.shape
    lon_count, lat_count = lax.axis_size("lon"), lax.axis_size("lat")
    slots = send_owner.shape[-1]
    groups = rows // PER
    hbm = pl.BlockSpec(memory_space=pltpu.HBM)
    smem = pl.BlockSpec(memory_space=pltpu.SMEM)
    f32 = jnp.float32
    blocks = channels // 8
    reach = LOW + rows + HIGH
    operands = (
        offsets.reshape(2, 1, rows // TILE), send_owner, send_cell, send_target, send_frac,
        fields.reshape(channels, rows, columns), fields.reshape(channels * rows, columns),
        fractions.reshape(2, rows, columns),
    )
    operands = [pltpu.with_memory_space_constraint(x, pltpu.HBM) for x in operands]
    operands.insert(1, send_count)
    out = pl.pallas_call(
        functools.partial(kernel, lon_count, lat_count, rows, channels, slots),
        out_shape=jax.ShapeDtypeStruct((channels * rows, columns), f32),
        in_specs=[hbm, smem] + [hbm] * 7,
        out_specs=pl.BlockSpec(memory_space=pltpu.VMEM),
        scratch_shapes=[
            pltpu.SMEM((2, 1, rows // TILE), jnp.int32),
            pltpu.SMEM(send_owner.shape, jnp.int32),
            pltpu.SMEM(send_cell.shape, jnp.int32),
            pltpu.SMEM(send_target.shape, jnp.int32),
            pltpu.SMEM(send_frac.shape, f32),
            pltpu.VMEM((channels * rows, columns), f32),
            pltpu.VMEM((2, rows, columns), f32),
            pltpu.VMEM((blocks, reach, 8, columns), f32),
            pltpu.VMEM((blocks, rows, 8, columns), f32),
            pltpu.VMEM((blocks, 8, LOW, columns), f32),
            pltpu.VMEM((blocks, 8, 8, columns), f32),
            pltpu.VMEM((blocks, 8, columns), f32),
            pltpu.VMEM((blocks, 8, columns), f32),
            pltpu.VMEM((groups, channels, columns), f32),
            pltpu.VMEM((groups, channels, columns), f32),
            pltpu.VMEM((2, groups + 3, channels, columns), f32),
            pltpu.VMEM((blocks, reach, 8, columns), f32),
            pltpu.VMEM((8, rows, columns), f32),
            pltpu.VMEM((4, slots, columns), f32),
            pltpu.VMEM((2, blocks, 8, columns), f32),
            pltpu.VMEM((lon_count, blocks, 8, columns), f32),
            pltpu.SemaphoreType.DMA((7,)),
            pltpu.SemaphoreType.DMA((2 * blocks + 7,)),
            pltpu.SemaphoreType.DMA((2 * blocks + 7,)),
            pltpu.SemaphoreType.DMA((2, blocks)),
            pltpu.SemaphoreType.DMA((lon_count, blocks)),
        ],
        compiler_params=pltpu.CompilerParams(
            collective_id=0, has_side_effects=True, vmem_limit_bytes=24 * 1024 * 1024
        ),
    )(*operands)
    return out.reshape(fields.shape)


def solution(mesh):
    placed = (
        P("panel", None, "lon", "lat"),
        P("panel", None, "lon", "lat"),
        P("panel", None, "lon", "lat"),
        P("panel", "lon", "lat"),
        P("panel", "lon", "lat", None),
        P("panel", "lon", "lat", None),
        P("panel", "lon", "lat", None),
        P("panel", "lon", "lat", None, None),
    )
    return jax.shard_map(
        body, mesh=mesh, in_specs=placed, out_specs=P("panel", None, "lon", "lat"), check_vma=False
    )
```

```python
import functools

import jax
import jax.numpy as jnp
from jax import lax
from jax.experimental import pallas as pl
from jax.experimental.pallas import tpu as pltpu
from jax.sharding import PartitionSpec as P

TILE = 8
LOW = 8
HIGH = 9
STRIP = 16
PER = 128 // STRIP
MESH = pl.DeviceIdType.MESH


def lagrange(x):
    return (
        -x * (x - 1.0) * (x - 2.0) * (1.0 / 6.0),
        (x + 1.0) * (x - 1.0) * (x - 2.0) * 0.5,
        -(x + 1.0) * x * (x - 2.0) * 0.5,
        (x + 1.0) * x * (x - 1.0) * (1.0 / 6.0),
    )


def kernel(
    lon_count, lat_count, rows, channels, slots,
    offsets_hbm, count, owner_hbm, cell_hbm, target_hbm, frac_hbm, x_hbm, tall_hbm, fractions_hbm, out_ref,
    offsets, owner, cell, cell_line, target, frac, x_ref, frac_ref,
    ext, adv, land_lo, land_hi, land_one, one_out, pack_l, pack_r, strips, halo, weights, slot_rows, rim_out, rim_in,
    in_sem, send_sem, recv_sem, rim_send, rim_recv,
):
    p = lax.axis_index("panel")
    i = lax.axis_index("lon")
    j = lax.axis_index("lat")
    groups = rows // PER
    blocks = channels // 8
    own = LOW
    from_r, from_l = strips.at[0], strips.at[1]
    has_prev, has_next = i > 0, i < lon_count - 1
    has_left, has_right = j > 0, j < lat_count - 1
    is_rim = jnp.logical_or(i == 0, i == lon_count - 1)

    around = [
        (-1, 0, has_prev), (1, 0, has_next), (0, -1, has_left), (0, 1, has_right),
        (-1, -1, has_prev & has_left), (1, -1, has_next & has_left),
        (-1, 1, has_prev & has_right), (1, 1, has_next & has_right),
    ]
    barrier = pltpu.get_barrier_semaphore()
    waits = jnp.int32(0)
    for di, dj, there in around:
        @pl.when(there)
        def _(di=di, dj=dj):
            pl.semaphore_signal(barrier, inc=1, device_id=(p, i + di, j + dj), device_id_type=MESH)
        waits = waits + there.astype(jnp.int32)

    @pl.when(is_rim)
    def _():
        def greet(m, carry):
            pl.semaphore_signal(barrier, inc=1, device_id=(1 - p, m, j), device_id_type=MESH)
            return carry
        lax.fori_loop(0, lon_count, greet, 0)

    @pl.when(jnp.logical_not(is_rim))
    def _():
        for m in (0, lon_count - 1):
            pl.semaphore_signal(barrier, inc=1, device_id=(1 - p, m, j), device_id_type=MESH)

    waits = waits + jnp.where(is_rim, lon_count, 2)

    loads = [
        pltpu.make_async_copy(src, dst, in_sem.at[n])
        for n, (src, dst) in enumerate([
            (tall_hbm, x_ref), (fractions_hbm, frac_ref), (offsets_hbm, offsets),
            (owner_hbm, owner), (cell_hbm, cell), (cell_hbm, cell_line), (target_hbm, target), (frac_hbm, frac),
        ])
    ]
    for load in loads:
        load.start()

    def clear(ref, start, size):
        ref[pl.ds(start, size)] = jnp.zeros((size,) + ref.shape[1:], jnp.float32)

    @pl.when(jnp.logical_not(has_prev))
    def _():
        clear(land_lo, 0, blocks)
        clear(from_r, 0, 1)
        clear(from_l, 0, 1)

    @pl.when(jnp.logical_not(has_next))
    def _():
        clear(land_hi, 0, blocks)
        clear(land_one, 0, blocks)
        clear(from_r, 1 + groups, 2)
        clear(from_l, 1 + groups, 2)

    @pl.when(jnp.logical_not(has_right))
    def _():
        clear(from_r, 0, groups + 3)

    @pl.when(jnp.logical_not(has_left))
    def _():
        clear(from_l, 0, groups + 3)

    lane = lax.broadcasted_iota(jnp.int32, (8, 128), 1)
    strip = lane // STRIP

    def pack(g):
        for c in range(blocks):
            left = jnp.zeros((8, 128), jnp.float32)
            right = jnp.zeros((8, 128), jnp.float32)
            for m in range(PER):
                row = g * PER + m
                v = x_ref[pl.ds(c * 8 * rows + row, 8, stride=rows), :]
                ext[c, own + row] = v
                rolled = pltpu.roll(v, STRIP * m, 1) if m else v
                left = jnp.where(strip == m, rolled, left)
                right = jnp.where(strip == (m + PER - 1) % PER, rolled, right)
            pack_l[g, pl.ds(c * 8, 8), :] = left
            pack_r[g, pl.ds(c * 8, 8), :] = right

    copies = []

    def send(src, dst, side):
        di, dj, there = around[side]
        n = len(copies)
        copy = pltpu.make_async_remote_copy(
            src_ref=src, dst_ref=dst, send_sem=send_sem.at[n], recv_sem=recv_sem.at[n],
            device_id=(p, i + di, j + dj), device_id_type=MESH,
        )
        arrives = [t for a, b, t in around if (a, b) == (-di, -dj)][0]
        copies.append((copy, there, arrives))
        pl.when(there)(copy.start)

    def arrive(n):
        copy, _, arrives = copies[n]
        pl.when(arrives)(copy.wait_recv)

    pl.semaphore_wait(barrier, waits)

    def send_tiles(c):
        part = pl.ds(c * 8, 8)
        send(x_hbm.at[part, pl.ds(0, 8), :], land_hi.at[c], 0)
        send(x_hbm.at[part, pl.ds(rows - LOW, LOW), :], land_lo.at[c], 1)

    send_tiles(0)
    loads[0].wait()
    for c in range(blocks):
        one_out[c] = x_ref[pl.ds(c * 8 * rows + 8, 8, stride=rows), :]
    send(one_out, land_one, 0)
    for c in range(1, blocks - 1):
        send_tiles(c)
    for g in range(groups):
        pack(g)
    send(pack_l, from_r.at[pl.ds(1, groups)], 2)
    send(pack_r, from_l.at[pl.ds(1, groups)], 3)
    send(pack_l.at[pl.ds(0, 2)], from_r.at[pl.ds(1 + groups, 2)], 4)
    send(pack_l.at[pl.ds(groups - 1, 1)], from_r.at[pl.ds(0, 1)], 5)
    send(pack_r.at[pl.ds(0, 2)], from_l.at[pl.ds(1 + groups, 2)], 6)
    send(pack_r.at[pl.ds(groups - 1, 1)], from_l.at[pl.ds(0, 1)], 7)
    send_tiles(blocks - 1)

    loads[1].wait()
    for g in range(groups):
        at = pl.ds(g * 8, 8)
        for axis in range(2):
            for n, w in enumerate(lagrange(frac_ref[axis, at, :])):
                weights[4 * axis + n, at, :] = w
    for load in loads[2:]:
        load.wait()

    live = count[0, 0, 0]
    f32 = jnp.float32
    diagonal = lax.broadcasted_iota(jnp.int32, (slots, slots), 0) == lax.broadcasted_iota(
        jnp.int32, (slots, slots), 1
    )

    def column(line):
        line = jnp.broadcast_to(line.astype(f32), (slots, slots))
        return jnp.sum(jnp.where(diagonal, line, 0.0), axis=1, keepdims=True)

    is_live = lax.broadcasted_iota(jnp.int32, (1, slots), 1) < live
    goal = jnp.where(is_live, target[0, 0], 128)
    to_first = owner[0, 0] == 0
    col = column(cell_line[0, 0] & 127)
    a, b = column(frac[0, 0, 0, pl.ds(0, 1), :]), column(frac[0, 0, 0, pl.ds(1, 1), :])
    place = lax.broadcasted_iota(jnp.int32, (slots, 128), 1).astype(f32)
    across = jnp.where(place == col, 1.0 - b, jnp.where(place == col + 1.0, b, 0.0))
    slot_rows[0] = (1.0 - a) * across
    slot_rows[1] = a * across
    slot_rows[2] = jnp.where(place == column(jnp.where(to_first, goal, 128)), 1.0, 0.0)
    slot_rows[3] = jnp.where(place == column(jnp.where(to_first, 128, goal)), 1.0, 0.0)

    side = jnp.where(has_right, 0, 1)
    kept = (lane < 64) == has_right

    def unpack(g, count):
        for c in range(blocks):
            at = pl.ds(c * 8, 8)
            for m in range(count):
                def turned(s):
                    v = strips[s, g, at, :]
                    return pltpu.roll(v, 128 - STRIP * m, 1) if m else v
                if lat_count == 2:
                    row = jnp.where(kept, turned(side), 0.0)
                else:
                    row = jnp.where(lane < 64, turned(0), turned(1))
                halo[c, g * PER + m] = row

    def tile(t, c):
        start = t * TILE + LOW - 1 + offsets[0, 0, t]
        shift = offsets[1, 0, t]
        inside, turn = [], []
        for b in range(4):
            k = shift + (b - 1)
            inside.append((lane >= k) & (lane < 128 + k))
            turn.append((256 - k) & 127)
        shifted = []
        for r in range(TILE):
            while len(shifted) < r + 4:
                main, edge = ext[c, start + len(shifted)], halo[c, start + len(shifted)]
                shifted.append(
                    [pltpu.roll(jnp.where(inside[b], main, edge), turn[b], 1) for b in range(4)]
                )
            row = t * TILE + r
            w = [jnp.broadcast_to(weights[n, pl.ds(row, 1), :], (8, 128)) for n in range(8)]
            total = None
            for a in range(4):
                inner = w[4] * shifted[r + a][0]
                for b in range(1, 4):
                    inner = inner + w[4 + b] * shifted[r + a][b]
                total = w[a] * inner if total is None else total + w[a] * inner
            adv[c, row] = total
            out_ref[pl.ds(c * 8 * rows + row, 8, stride=rows), :] = total

    def donate(c, k, carry):
        first, last = carry
        row = cell[0, 0, 0, k] >> 7
        at = pl.ds(k, 1)
        mixed = slot_rows[0, at, :] * adv[c, row] + slot_rows[1, at, :] * adv[c, row + 1]
        value = jnp.sum(mixed, axis=1, keepdims=True)
        return first + slot_rows[2, at, :] * value, last + slot_rows[3, at, :] * value

    tiles = rows // TILE
    one, lat = 2, 2 * blocks + 1 - 2
    corners, last_tiles = lat + 2, lat + 6
    for n in (lat, lat + 1):
        arrive(n)
    for g in range(1, 1 + groups):
        unpack(g, PER)
    for c in range(blocks):
        for t in range(1, tiles - 2):
            tile(t, c)
    for n in range(corners, corners + 4):
        arrive(n)
    unpack(0, PER)
    unpack(1 + groups, PER)
    unpack(2 + groups, 1)
    zero = jnp.zeros((8, 128), jnp.float32)
    sends = []
    for c in range(blocks):
        at = 0 if c == 0 else last_tiles if c == blocks - 1 else 2 * c + 1
        arrive(at)
        arrive(at + 1)
        if c == 0:
            arrive(one)
        ext[c, pl.ds(0, LOW)] = jnp.swapaxes(land_lo[c], 0, 1)
        ext[c, pl.ds(own + rows, 8)] = jnp.swapaxes(land_hi[c], 0, 1)
        ext[c, own + rows + 8] = land_one[c]
        for t in [0] + list(range(max(1, tiles - 2), tiles)):
            tile(t, c)
        first, last = lax.fori_loop(0, slots, functools.partial(donate, c), (zero, zero), unroll=slots)
        rim_out[0, c] = first
        rim_out[1, c] = last
        for n, m in enumerate((0, lon_count - 1)):
            copy = pltpu.make_async_remote_copy(
                src_ref=rim_out.at[n, c], dst_ref=rim_in.at[i, c], send_sem=rim_send.at[n, c],
                recv_sem=rim_recv.at[i, c], device_id=(1 - p, m, j), device_id_type=MESH,
            )
            copy.start()
            sends.append(copy)

    @pl.when(is_rim)
    def _():
        rim_row = jnp.where(i == 0, 0, rows - 1)
        for c in range(blocks):
            total = zero
            for m in range(lon_count):
                pltpu.make_async_remote_copy(
                    src_ref=rim_out.at[0, c], dst_ref=rim_in.at[m, c], send_sem=rim_send.at[0, c],
                    recv_sem=rim_recv.at[m, c], device_id=(1 - p, m, j), device_id_type=MESH,
                ).wait_recv()
                total = total + rim_in[m, c]
            out_ref[pl.ds(c * 8 * rows + rim_row, 8, stride=rows), :] = total

    for copy, there, _ in copies:
        pl.when(there)(copy.wait_send)
    for copy in sends:
        copy.wait_send()


def body(fields, offsets, fractions, send_count, send_owner, send_cell, send_target, send_frac):
    _, channels, rows, columns = fields.shape
    lon_count, lat_count = lax.axis_size("lon"), lax.axis_size("lat")
    slots = send_owner.shape[-1]
    groups = rows // PER
    hbm = pl.BlockSpec(memory_space=pltpu.HBM)
    smem = pl.BlockSpec(memory_space=pltpu.SMEM)
    f32 = jnp.float32
    blocks = channels // 8
    reach = LOW + rows + HIGH
    operands = (
        offsets.reshape(2, 1, rows // TILE), send_owner, send_cell, send_target, send_frac,
        fields.reshape(channels, rows, columns), fields.reshape(channels * rows, columns),
        fractions.reshape(2, rows, columns),
    )
    operands = [pltpu.with_memory_space_constraint(x, pltpu.HBM) for x in operands]
    operands.insert(1, send_count)
    out = pl.pallas_call(
        functools.partial(kernel, lon_count, lat_count, rows, channels, slots),
        out_shape=jax.ShapeDtypeStruct((channels * rows, columns), f32),
        in_specs=[hbm, smem] + [hbm] * 7,
        out_specs=pl.BlockSpec(memory_space=pltpu.VMEM),
        scratch_shapes=[
            pltpu.SMEM((2, 1, rows // TILE), jnp.int32),
            pltpu.VMEM(send_owner.shape, jnp.int32),
            pltpu.SMEM(send_cell.shape, jnp.int32),
            pltpu.VMEM(send_cell.shape, jnp.int32),
            pltpu.VMEM(send_target.shape, jnp.int32),
            pltpu.VMEM(send_frac.shape, f32),
            pltpu.VMEM((channels * rows, columns), f32),
            pltpu.VMEM((2, rows, columns), f32),
            pltpu.VMEM((blocks, reach, 8, columns), f32),
            pltpu.VMEM((blocks, rows, 8, columns), f32),
            pltpu.VMEM((blocks, 8, LOW, columns), f32),
            pltpu.VMEM((blocks, 8, 8, columns), f32),
            pltpu.VMEM((blocks, 8, columns), f32),
            pltpu.VMEM((blocks, 8, columns), f32),
            pltpu.VMEM((groups, channels, columns), f32),
            pltpu.VMEM((groups, channels, columns), f32),
            pltpu.VMEM((2, groups + 3, channels, columns), f32),
            pltpu.VMEM((blocks, reach, 8, columns), f32),
            pltpu.VMEM((8, rows, columns), f32),
            pltpu.VMEM((4, slots, columns), f32),
            pltpu.VMEM((2, blocks, 8, columns), f32),
            pltpu.VMEM((lon_count, blocks, 8, columns), f32),
            pltpu.SemaphoreType.DMA((8,)),
            pltpu.SemaphoreType.DMA((2 * blocks + 7,)),
            pltpu.SemaphoreType.DMA((2 * blocks + 7,)),
            pltpu.SemaphoreType.DMA((2, blocks)),
            pltpu.SemaphoreType.DMA((lon_count, blocks)),
        ],
        compiler_params=pltpu.CompilerParams(
            collective_id=0, has_side_effects=True, vmem_limit_bytes=24 * 1024 * 1024
        ),
    )(*operands)
    return out.reshape(fields.shape)


def solution(mesh):
    placed = (
        P("panel", None, "lon", "lat"),
        P("panel", None, "lon", "lat"),
        P("panel", None, "lon", "lat"),
        P("panel", "lon", "lat"),
        P("panel", "lon", "lat", None),
        P("panel", "lon", "lat", None),
        P("panel", "lon", "lat", None),
        P("panel", "lon", "lat", None, None),
    )
    return jax.shard_map(
        body, mesh=mesh, in_specs=placed, out_specs=P("panel", None, "lon", "lat"), check_vma=False
    )
```

```python
import functools

import jax
import jax.numpy as jnp
from jax import lax
from jax.experimental import pallas as pl
from jax.experimental.pallas import tpu as pltpu
from jax.sharding import PartitionSpec as P

TILE = 8
LOW = 8
HIGH = 9
STRIP = 16
PER = 128 // STRIP
MESH = pl.DeviceIdType.MESH


def lagrange(x):
    return (
        -x * (x - 1.0) * (x - 2.0) * (1.0 / 6.0),
        (x + 1.0) * (x - 1.0) * (x - 2.0) * 0.5,
        -(x + 1.0) * x * (x - 2.0) * 0.5,
        (x + 1.0) * x * (x - 1.0) * (1.0 / 6.0),
    )


def kernel(
    lon_count, lat_count, rows, channels, slots,
    offsets_hbm, count, owner_hbm, cell_hbm, target_hbm, frac_hbm, x_hbm, tall_hbm, fractions_hbm, out_ref,
    offsets, owner, cell, cell_line, target, frac, x_ref, frac_ref,
    ext, adv, land_lo, land_hi, land_one, one_out, pack_l, pack_r, strips, halo, weights, slot_rows, rim_out, rim_in,
    in_sem, send_sem, recv_sem, rim_send, rim_recv,
):
    p = lax.axis_index("panel")
    i = lax.axis_index("lon")
    j = lax.axis_index("lat")
    groups = rows // PER
    blocks = channels // 8
    own = LOW
    from_r, from_l = strips.at[0], strips.at[1]
    has_prev, has_next = i > 0, i < lon_count - 1
    has_left, has_right = j > 0, j < lat_count - 1
    is_rim = jnp.logical_or(i == 0, i == lon_count - 1)

    around = [
        (-1, 0, has_prev), (1, 0, has_next), (0, -1, has_left), (0, 1, has_right),
        (-1, -1, has_prev & has_left), (1, -1, has_next & has_left),
        (-1, 1, has_prev & has_right), (1, 1, has_next & has_right),
    ]
    barrier = pltpu.get_barrier_semaphore()
    waits = jnp.int32(0)
    for di, dj, there in around:
        @pl.when(there)
        def _(di=di, dj=dj):
            pl.semaphore_signal(barrier, inc=1, device_id=(p, i + di, j + dj), device_id_type=MESH)
        waits = waits + there.astype(jnp.int32)

    @pl.when(is_rim)
    def _():
        def greet(m, carry):
            pl.semaphore_signal(barrier, inc=1, device_id=(1 - p, m, j), device_id_type=MESH)
            return carry
        lax.fori_loop(0, lon_count, greet, 0)

    @pl.when(jnp.logical_not(is_rim))
    def _():
        for m in (0, lon_count - 1):
            pl.semaphore_signal(barrier, inc=1, device_id=(1 - p, m, j), device_id_type=MESH)

    waits = waits + jnp.where(is_rim, lon_count, 2)

    loads = [
        pltpu.make_async_copy(src, dst, in_sem.at[n])
        for n, (src, dst) in enumerate([
            (tall_hbm, x_ref), (fractions_hbm, frac_ref), (offsets_hbm, offsets),
            (owner_hbm, owner), (cell_hbm, cell), (cell_hbm, cell_line), (target_hbm, target), (frac_hbm, frac),
        ])
    ]
    for load in loads:
        load.start()

    def clear(ref, start, size):
        ref[pl.ds(start, size)] = jnp.zeros((size,) + ref.shape[1:], jnp.float32)

    @pl.when(jnp.logical_not(has_prev))
    def _():
        clear(land_lo, 0, blocks)
        clear(from_r, 0, 1)
        clear(from_l, 0, 1)

    @pl.when(jnp.logical_not(has_next))
    def _():
        clear(land_hi, 0, blocks)
        clear(land_one, 0, blocks)
        clear(from_r, 1 + groups, 2)
        clear(from_l, 1 + groups, 2)

    @pl.when(jnp.logical_not(has_right))
    def _():
        clear(from_r, 0, groups + 3)

    @pl.when(jnp.logical_not(has_left))
    def _():
        clear(from_l, 0, groups + 3)

    lane = lax.broadcasted_iota(jnp.int32, (8, 128), 1)
    strip = lane // STRIP

    def pack(g):
        for c in range(blocks):
            left = jnp.zeros((8, 128), jnp.float32)
            right = jnp.zeros((8, 128), jnp.float32)
            for m in range(PER):
                row = g * PER + m
                v = x_ref[pl.ds(c * 8 * rows + row, 8, stride=rows), :]
                ext[c, own + row] = v
                rolled = pltpu.roll(v, STRIP * m, 1) if m else v
                left = jnp.where(strip == m, rolled, left)
                right = jnp.where(strip == (m + PER - 1) % PER, rolled, right)
            pack_l[g, pl.ds(c * 8, 8), :] = left
            pack_r[g, pl.ds(c * 8, 8), :] = right

    copies = []

    def send(src, dst, side):
        di, dj, there = around[side]
        n = len(copies)
        copy = pltpu.make_async_remote_copy(
            src_ref=src, dst_ref=dst, send_sem=send_sem.at[n], recv_sem=recv_sem.at[n],
            device_id=(p, i + di, j + dj), device_id_type=MESH,
        )
        arrives = [t for a, b, t in around if (a, b) == (-di, -dj)][0]
        copies.append((copy, there, arrives))
        pl.when(there)(copy.start)

    def arrive(n):
        copy, _, arrives = copies[n]
        pl.when(arrives)(copy.wait_recv)

    pl.semaphore_wait(barrier, waits)

    def send_tiles(c):
        part = pl.ds(c * 8, 8)
        send(x_hbm.at[part, pl.ds(0, 8), :], land_hi.at[c], 0)
        send(x_hbm.at[part, pl.ds(rows - LOW, LOW), :], land_lo.at[c], 1)

    send_tiles(0)
    loads[0].wait()
    for c in range(blocks):
        one_out[c] = x_ref[pl.ds(c * 8 * rows + 8, 8, stride=rows), :]
    send(one_out, land_one, 0)
    for c in range(1, blocks - 1):
        send_tiles(c)
    for g in range(groups):
        pack(g)
    send(pack_l, from_r.at[pl.ds(1, groups)], 2)
    send(pack_r, from_l.at[pl.ds(1, groups)], 3)
    send(pack_l.at[pl.ds(0, 2)], from_r.at[pl.ds(1 + groups, 2)], 4)
    send(pack_l.at[pl.ds(groups - 1, 1)], from_r.at[pl.ds(0, 1)], 5)
    send(pack_r.at[pl.ds(0, 2)], from_l.at[pl.ds(1 + groups, 2)], 6)
    send(pack_r.at[pl.ds(groups - 1, 1)], from_l.at[pl.ds(0, 1)], 7)
    send_tiles(blocks - 1)

    loads[1].wait()
    for g in range(groups):
        at = pl.ds(g * 8, 8)
        for axis in range(2):
            for n, w in enumerate(lagrange(frac_ref[axis, at, :])):
                weights[4 * axis + n, at, :] = w
    for load in loads[2:]:
        load.wait()

    live = count[0, 0, 0]
    f32 = jnp.float32
    diagonal = lax.broadcasted_iota(jnp.int32, (slots, slots), 0) == lax.broadcasted_iota(
        jnp.int32, (slots, slots), 1
    )

    def column(line):
        line = jnp.broadcast_to(line.astype(f32), (slots, slots))
        return jnp.sum(jnp.where(diagonal, line, 0.0), axis=1, keepdims=True)

    is_live = lax.broadcasted_iota(jnp.int32, (1, slots), 1) < live
    goal = jnp.where(is_live, target[0, 0], 128)
    to_first = owner[0, 0] == 0
    col = column(cell_line[0, 0] & 127)
    a, b = column(frac[0, 0, 0, pl.ds(0, 1), :]), column(frac[0, 0, 0, pl.ds(1, 1), :])
    place = lax.broadcasted_iota(jnp.int32, (slots, 128), 1).astype(f32)
    across = jnp.where(place == col, 1.0 - b, jnp.where(place == col + 1.0, b, 0.0))
    slot_rows[0] = (1.0 - a) * across
    slot_rows[1] = a * across
    slot_rows[2] = jnp.where(place == column(jnp.where(to_first, goal, 128)), 1.0, 0.0)
    slot_rows[3] = jnp.where(place == column(jnp.where(to_first, 128, goal)), 1.0, 0.0)

    side = jnp.where(has_right, 0, 1)
    kept = (lane < 64) == has_right

    def unpack(g, count):
        for c in range(blocks):
            at = pl.ds(c * 8, 8)
            for m in range(count):
                def turned(s):
                    v = strips[s, g, at, :]
                    return pltpu.roll(v, 128 - STRIP * m, 1) if m else v
                if lat_count == 2:
                    row = jnp.where(kept, turned(side), 0.0)
                else:
                    row = jnp.where(lane < 64, turned(0), turned(1))
                halo[c, g * PER + m] = row

    def tile(t, c):
        start = t * TILE + LOW - 1 + offsets[0, 0, t]
        shift = offsets[1, 0, t]
        inside, turn = [], []
        for b in range(4):
            k = shift + (b - 1)
            inside.append((lane >= k) & (lane < 128 + k))
            turn.append((256 - k) & 127)
        shifted = []
        for r in range(TILE):
            while len(shifted) < r + 4:
                main, edge = ext[c, start + len(shifted)], halo[c, start + len(shifted)]
                shifted.append(
                    [pltpu.roll(jnp.where(inside[b], main, edge), turn[b], 1) for b in range(4)]
                )
            row = t * TILE + r
            w = [jnp.broadcast_to(weights[n, pl.ds(row, 1), :], (8, 128)) for n in range(8)]
            total = None
            for a in range(4):
                inner = w[4] * shifted[r + a][0]
                for b in range(1, 4):
                    inner = inner + w[4 + b] * shifted[r + a][b]
                total = w[a] * inner if total is None else total + w[a] * inner
            adv[c, row] = total
            out_ref[pl.ds(c * 8 * rows + row, 8, stride=rows), :] = total

    def donate(c, k, carry):
        first, last = carry
        row = cell[0, 0, 0, k] >> 7
        at = pl.ds(k, 1)
        mixed = slot_rows[0, at, :] * adv[c, row] + slot_rows[1, at, :] * adv[c, row + 1]
        value = jnp.sum(mixed, axis=1, keepdims=True)
        return first + slot_rows[2, at, :] * value, last + slot_rows[3, at, :] * value

    tiles = rows // TILE
    one, lat = 2, 2 * blocks + 1 - 2
    corners, last_tiles = lat + 2, lat + 6
    for n in (lat, lat + 1):
        arrive(n)
    for g in range(1, 1 + groups):
        unpack(g, PER)
    for c in range(blocks):
        for t in range(1, tiles - 2):
            tile(t, c)
    for n in range(corners, corners + 4):
        arrive(n)
    unpack(0, PER)
    unpack(1 + groups, PER)
    unpack(2 + groups, 1)
    zero = jnp.zeros((8, 128), jnp.float32)
    sends = []
    for c in range(blocks):
        at = 0 if c == 0 else last_tiles if c == blocks - 1 else 2 * c + 1
        arrive(at)
        arrive(at + 1)
        if c == 0:
            arrive(one)
        ext[c, pl.ds(0, LOW)] = jnp.swapaxes(land_lo[c], 0, 1)
        ext[c, pl.ds(own + rows, 8)] = jnp.swapaxes(land_hi[c], 0, 1)
        ext[c, own + rows + 8] = land_one[c]
        for t in [0] + list(range(max(1, tiles - 2), tiles)):
            tile(t, c)
        first, last = lax.fori_loop(0, slots, functools.partial(donate, c), (zero, zero), unroll=slots)
        rim_out[0, c] = first
        rim_out[1, c] = last
        for n, m in enumerate((0, lon_count - 1)):
            copy = pltpu.make_async_remote_copy(
                src_ref=rim_out.at[n, c], dst_ref=rim_in.at[i, c], send_sem=rim_send.at[n, c],
                recv_sem=rim_recv, device_id=(1 - p, m, j), device_id_type=MESH,
            )
            copy.start()
            sends.append(copy)

    for copy, there, _ in copies:
        pl.when(there)(copy.wait_send)
    for copy in sends:
        copy.wait_send()

    @pl.when(is_rim)
    def _():
        rim_row = jnp.where(i == 0, 0, rows - 1)
        pltpu.make_async_remote_copy(
            src_ref=rim_in, dst_ref=rim_in, send_sem=rim_send.at[0, 0], recv_sem=rim_recv,
            device_id=(1 - p, i, j), device_id_type=MESH,
        ).wait_recv()
        for c in range(blocks):
            total = rim_in[0, c]
            for m in range(1, lon_count):
                total = total + rim_in[m, c]
            out_ref[pl.ds(c * 8 * rows + rim_row, 8, stride=rows), :] = total


def body(fields, offsets, fractions, send_count, send_owner, send_cell, send_target, send_frac):
    _, channels, rows, columns = fields.shape
    lon_count, lat_count = lax.axis_size("lon"), lax.axis_size("lat")
    slots = send_owner.shape[-1]
    groups = rows // PER
    hbm = pl.BlockSpec(memory_space=pltpu.HBM)
    smem = pl.BlockSpec(memory_space=pltpu.SMEM)
    f32 = jnp.float32
    blocks = channels // 8
    reach = LOW + rows + HIGH
    operands = (
        offsets.reshape(2, 1, rows // TILE), send_owner, send_cell, send_target, send_frac,
        fields.reshape(channels, rows, columns), fields.reshape(channels * rows, columns),
        fractions.reshape(2, rows, columns),
    )
    operands = [pltpu.with_memory_space_constraint(x, pltpu.HBM) for x in operands]
    operands.insert(1, send_count)
    out = pl.pallas_call(
        functools.partial(kernel, lon_count, lat_count, rows, channels, slots),
        out_shape=jax.ShapeDtypeStruct((channels * rows, columns), f32),
        in_specs=[hbm, smem] + [hbm] * 7,
        out_specs=pl.BlockSpec(memory_space=pltpu.VMEM),
        scratch_shapes=[
            pltpu.SMEM((2, 1, rows // TILE), jnp.int32),
            pltpu.VMEM(send_owner.shape, jnp.int32),
            pltpu.SMEM(send_cell.shape, jnp.int32),
            pltpu.VMEM(send_cell.shape, jnp.int32),
            pltpu.VMEM(send_target.shape, jnp.int32),
            pltpu.VMEM(send_frac.shape, f32),
            pltpu.VMEM((channels * rows, columns), f32),
            pltpu.VMEM((2, rows, columns), f32),
            pltpu.VMEM((blocks, reach, 8, columns), f32),
            pltpu.VMEM((blocks, rows, 8, columns), f32),
            pltpu.VMEM((blocks, 8, LOW, columns), f32),
            pltpu.VMEM((blocks, 8, 8, columns), f32),
            pltpu.VMEM((blocks, 8, columns), f32),
            pltpu.VMEM((blocks, 8, columns), f32),
            pltpu.VMEM((groups, channels, columns), f32),
            pltpu.VMEM((groups, channels, columns), f32),
            pltpu.VMEM((2, groups + 3, channels, columns), f32),
            pltpu.VMEM((blocks, reach, 8, columns), f32),
            pltpu.VMEM((8, rows, columns), f32),
            pltpu.VMEM((4, slots, columns), f32),
            pltpu.VMEM((2, blocks, 8, columns), f32),
            pltpu.VMEM((lon_count, blocks, 8, columns), f32),
            pltpu.SemaphoreType.DMA((8,)),
            pltpu.SemaphoreType.DMA((2 * blocks + 7,)),
            pltpu.SemaphoreType.DMA((2 * blocks + 7,)),
            pltpu.SemaphoreType.DMA((2, blocks)),
            pltpu.SemaphoreType.DMA(()),
        ],
        compiler_params=pltpu.CompilerParams(
            collective_id=0, has_side_effects=True, vmem_limit_bytes=24 * 1024 * 1024
        ),
    )(*operands)
    return out.reshape(fields.shape)


def solution(mesh):
    placed = (
        P("panel", None, "lon", "lat"),
        P("panel", None, "lon", "lat"),
        P("panel", None, "lon", "lat"),
        P("panel", "lon", "lat"),
        P("panel", "lon", "lat", None),
        P("panel", "lon", "lat", None),
        P("panel", "lon", "lat", None),
        P("panel", "lon", "lat", None, None),
    )
    return jax.shard_map(
        body, mesh=mesh, in_specs=placed, out_specs=P("panel", None, "lon", "lat"), check_vma=False
    )
```
